256 devices in a mesh: ctx: 32 (over y, z_hi, x), head: 8 (over z_lo, core).
Axes of the slice: x: 4, y: 4, z: 8 (z_hi: 2, z_lo: 4; z = z_hi * 4 + z_lo), core: 2. Of those that a mesh axis runs over, the one named last changes fastest.
Arguments:
- queries: bfloat16 [8192, 1024], P('ctx', 'head'), may hold values from -10 to 10
- keys: bfloat16 [8192, 128], P('ctx'), may hold values from -6 to 6
- values: bfloat16 [8192, 128], P('ctx'), may hold values from -6 to 6
- doc_lengths: int32 [4], replicated, may hold values from 1 to 6144, 8192 in all
Outputs:
- attn_rows: bfloat16 [8192, 1024], P('ctx', 'head')
- col_scores: float32 [8192], P(('ctx', 'head'))
The draws below stay inside these ranges and needn't reach their ends.
Inputs may be any that keep to these rules, and one draw needn't show every extreme that they name: `doc_lengths`: the 4 lengths sum to 8192 and the longest is exactly 6144.
All inputs are finite; a program needn't handle non-finite values.
Results may differ from the reference program's by a relative error of at most 0.0075.
Values may be sent and summed in bfloat16 or wider, within the bound.
No kernel may reach another device: no remote copies, remote signals or barrier semaphores. Data moves between devices by JAX's collectives and lax.ppermute only.
A program may use at most 64 MiB of HBM per device.

```python
import math
import jax
import jax.numpy as jnp
import numpy as np
from jax import lax

HD = 128
HEADS = 8
SEQS = 4
TOK_DEV = 256
TOKENS = 8192


def draw_queries(key, part):
    key = jax.random.fold_in(key, 11)
    result = 2.5 * jax.random.truncated_normal(key, -4.0, 4.0, (TOKENS, HEADS * HD))
    return result.astype(jnp.float32).astype(jnp.bfloat16)


def draw_keys(key, part):
    key = jax.random.fold_in(key, 23)
    result = jax.random.truncated_normal(key, -6.0, 6.0, (TOKENS, HD))
    return result.astype(jnp.float32).astype(jnp.bfloat16)


def levels(key, extent, cuts, smallest, largest):
    gain, own = 1.0, jax.random.fold_in(key, 6)
    for position, blocks in cuts:
        heights = jnp.exp(jax.random.uniform(jax.random.fold_in(own, position), (blocks,), jnp.float32, smallest / len(cuts), largest / len(cuts)))
        gain = gain * jnp.repeat(heights, extent[position] // blocks).reshape([-1 if axis == position else 1 for axis in range(len(extent))])
    return gain


def split_up(count, total, reach, lean):
    portions = [(1 << 20) // math.isqrt(rank ** lean) + 1 for rank in range(2, count + 1)]
    rest, counts = total - reach - (count - 1), [1] * (count - 1)
    while rest > 0:
        movable = [i for i in range(count - 1) if counts[i] < reach]
        whole, remaining = sum([portions[i] for i in movable]), rest
        for i in movable:
            more = min(reach - counts[i], max(1, remaining * portions[i] // whole), rest)
            counts[i] = counts[i] + more
            rest = rest - more
    return np.array([reach] + counts)


def uneven(own_key, amount, total, bound, skew):
    if amount == 2:
        one = jax.random.randint(own_key, (), max(1, total - bound), min(bound, total - 1) + 1)
        return jnp.stack([one, total - one])
    sizes = jnp.asarray(split_up(amount, total, bound, skew), jnp.int32)
    twos = (amount - 1) // 2
    source_of, taker = sizes[1:1 + 2 * twos:2], sizes[2:2 + 2 * twos:2]
    slack = jnp.minimum(source_of - 1, bound - taker)
    shifted = jax.random.randint(jax.random.fold_in(own_key, 1), (twos,), 0, 1 << 20) % (slack + 1)
    sizes = sizes.at[1:1 + 2 * twos:2].set(source_of - shifted).at[2:2 + 2 * twos:2].set(taker + shifted)
    return sizes[jax.random.permutation(jax.random.fold_in(own_key, 2), amount)]


def gaussian(stream_key, extent, scale, reach, shards=(), held_as=jnp.bfloat16):
    gain = levels(stream_key, extent, shards, -0.22, 0.18) if shards else 1.0
    values = jax.random.normal(stream_key, extent, jnp.float32) * scale * gain
    return jnp.minimum(jnp.maximum(values, -reach), reach).astype(held_as)


def setup_inputs(seed: int = 0) -> dict:
    key_list = jax.random.split(jax.random.key(seed), 5)
    queries = draw_queries(jax.random.fold_in(key_list[4], 71), 0)
    keys = draw_keys(jax.random.fold_in(key_list[4], 71), 0)
    values = gaussian(key_list[2], (TOKENS, HD), 1.0, 6.0, ((0, 32),))
    doc_lengths = uneven(key_list[3], SEQS, TOKENS, 3 * TOKENS // 4, 2).astype(jnp.int32)
    return {"queries": queries, "keys": keys, "values": values, "doc_lengths": doc_lengths}


def doc_index(doc_lengths, positions):
    doc_ends = jnp.cumsum(doc_lengths)
    return lax.optimization_barrier(jnp.sum((positions[:, None] >= doc_ends[None, :]).astype(jnp.int32), axis=1))

def reference(queries, keys, values, doc_lengths):
    inv_root = 1.0 / math.sqrt(HD)
    positions = jnp.arange(TOKENS, dtype=jnp.int32)
    key_docs = doc_index(doc_lengths, positions)
    per_block = queries.reshape(TOKENS // TOK_DEV, TOK_DEV, HEADS, HD)

    def one_block(block_index):
        q_block = per_block[block_index]
        q_pos = block_index * TOK_DEV + jnp.arange(TOK_DEV, dtype=jnp.int32)
        q_docs = doc_index(doc_lengths, q_pos)
        allowed = (key_docs[None, :] == q_docs[:, None]) & (positions[None, :] <= q_pos[:, None])

        def one_head(head_index):
            q_rows = q_block[:, head_index, :]
            logits = jnp.dot(q_rows, keys.T, preferred_element_type=jnp.float32) * inv_root
            logits = jnp.where(allowed, logits, -jnp.inf)
            row_max = lax.optimization_barrier(jnp.max(logits, axis=1, keepdims=True))
            log_norm = row_max + jnp.log(lax.optimization_barrier(jnp.sum(jnp.exp(logits - row_max), axis=1, keepdims=True)))
            probs = jnp.exp(logits - log_norm)
            rows_out = jnp.dot(probs.astype(jnp.bfloat16), values, preferred_element_type=jnp.float32).astype(jnp.bfloat16)
            return (rows_out, lax.optimization_barrier(jnp.sum(probs, axis=0)))
        head_rows, head_cols = lax.map(one_head, jnp.arange(HEADS, dtype=jnp.int32))
        return (head_rows, lax.optimization_barrier(jnp.sum(head_cols, axis=0)))
    block_rows, block_cols = lax.map(one_block, jnp.arange(TOKENS // TOK_DEV, dtype=jnp.int32))
    attn_rows = block_rows.transpose(0, 2, 1, 3).reshape(TOKENS, HEADS * HD)
    col_scores = lax.optimization_barrier(jnp.sum(block_cols, axis=0)) / HEADS
    return (attn_rows, col_scores)
```

```python
import functools
import math

import jax
import jax.numpy as jnp
from jax import lax
from jax.experimental import pallas as pl
from jax.experimental.pallas import tpu as pltpu
from jax.sharding import Mesh, PartitionSpec as P

HD = 128
HEADS = 8
NY, NZH, NX, NZL, NC = 4, 2, 4, 4, 2
TOK = 256
CHUNK = TOK // HEADS
PER = TOK // NC
KEYS = NY * NX * PER
ROWS = 4 * TOK
SCALE = math.log2(math.e) / math.sqrt(HD)
TILE = 256
MIB = 1024 * 1024


def vmem(count=None):
    spec = pl.BlockSpec(memory_space=pltpu.VMEM)
    return spec if count is None else [spec] * count


def score_kernel(place_ref, docs_ref, keys_ref, q0, q1, q2, q3, probs_ref, stats_ref, raw_ref, q_ref):
    for i, q in enumerate((q0, q1, q2, q3)):
        q_ref[pl.ds(i * TOK, TOK), :] = q[...]
    y, zh, x, c = place_ref[0], place_ref[1], place_ref[2], place_ref[3]
    e0 = docs_ref[0]
    e1 = e0 + docs_ref[1]
    e2 = e1 + docs_ref[2]
    own = (y * 8 + zh * 4 + x) * TOK
    other = (y * 8 + (1 - zh) * 4 + x) * TOK
    lane = lax.broadcasted_iota(jnp.int32, (1, ROWS), 1)
    pos = jnp.where(lane < 2 * TOK, own, other) + lax.rem(lane, TOK)
    start = jnp.zeros_like(pos)
    for end in (e0, e1, e2):
        start = jnp.where(pos >= end, end, start)

    def first(t, peak):
        block = keys_ref[pl.ds(pl.multiple_of(t * TILE, TILE), TILE), :]
        raw = lax.dot_general(block, q_ref[...], (((1,), (1,)), ((), ())), preferred_element_type=jnp.float32)
        g = t * TILE + lax.broadcasted_iota(jnp.int32, (TILE, 1), 0)
        source = g // PER
        key_pos = (
            ((source // NX) * 8 + zh * 4 + source % NX) * TOK
            + ((g // CHUNK) % NZL * 2 + c) * CHUNK
            + g % CHUNK
        )
        raw = jnp.where((key_pos >= start) & (key_pos <= pos), raw, -jnp.inf)
        raw_ref[pl.ds(pl.multiple_of(t * TILE, TILE), TILE), :] = raw
        return jnp.maximum(peak, jnp.max(raw.reshape(TILE // 8, 8, ROWS), axis=0))

    peak = lax.fori_loop(0, KEYS // TILE, first, jnp.full((8, ROWS), -1e30, jnp.float32))
    row_max = jnp.max(peak, axis=0, keepdims=True)

    def second(t, total):
        rows = pl.ds(pl.multiple_of(t * TILE, TILE), TILE)
        probs = jnp.exp2((raw_ref[rows, :] - row_max) * SCALE)
        probs_ref[rows, :] = probs.astype(jnp.bfloat16)
        return total + jnp.sum(probs.reshape(TILE // 8, 8, ROWS), axis=0)

    total = lax.fori_loop(0, KEYS // TILE, second, jnp.zeros((8, ROWS), jnp.float32))
    stats_ref[0:1, :] = row_max
    stats_ref[1:2, :] = jnp.sum(total, axis=0, keepdims=True)


def column_kernel(probs_ref, s0, s1, s2, s3, cols_ref, weight_ref):
    def aligned(ref, flip):
        pieces = [ref[:, pl.ds((k ^ flip) * TOK, TOK)] for k in range(4)]
        both = jnp.concatenate(pieces, axis=1)
        return both[0:1, :], both[1:2, :]

    parts = [aligned(s, flip) for s, flip in ((s0, 0), (s1, 1), (s2, 2), (s3, 3))]
    top = functools.reduce(jnp.maximum, [m for m, _ in parts])
    norm = sum(l * jnp.exp2((m - top) * SCALE) for m, l in parts)
    weight = jnp.exp2((parts[0][0] - top) * SCALE) / norm
    weight_ref[...] = weight
    high = weight.astype(jnp.bfloat16).astype(jnp.float32)
    row = lax.broadcasted_iota(jnp.int32, (8, ROWS), 0)
    both = jnp.where(row == 0, high, jnp.where(row == 1, weight - high, 0.0)).astype(jnp.bfloat16)
    for k in range(NY * NX):
        sums = lax.dot_general(
            both, probs_ref[pl.ds(k * PER, PER), :], (((1,), (1,)), ((), ())), preferred_element_type=jnp.float32
        )
        line = jnp.sum(sums, axis=0, keepdims=True)
        cols_ref[pl.ds(k * NZL, NZL), :] = jnp.broadcast_to(line, (NZL, PER))


def value_kernel(probs_ref, values_ref, weight_ref, keep_ref, send_ref):
    acc = lax.dot_general(
        values_ref[...], probs_ref[...], (((0,), (0,)), ((), ())), preferred_element_type=jnp.float32
    )
    acc = acc * weight_ref[...]
    for k in range(2):
        keep_ref[k] = acc[:, (2 * k) * TOK : (2 * k + 1) * TOK]
        send_ref[k] = acc[:, (2 * k + 1) * TOK : (2 * k + 2) * TOK]


def body(queries, keys, values, doc_lengths):
    zc = ("zh", "zl", "c")
    place = jnp.stack([lax.axis_index(a) for a in ("y", "zh", "x", "c")]).astype(jnp.int32)
    c = lax.axis_index("c")

    def across(x):
        return lax.ppermute(x, "c", [(0, 1), (1, 0)])

    def partner(x, flip=12):
        return lax.ppermute(x, zc, [(i, i ^ flip) for i in range(16)])

    both = jnp.stack([keys, values]).reshape(2, NZL, NC, CHUNK, HD)
    mine = jnp.where(c == 0, both[:, :, 0], both[:, :, 1]).reshape(2, PER, HD)
    parts = lax.all_to_all(jnp.broadcast_to(mine[None], (NY * NX, 2, PER, HD)), ("y", "x"), 0, 0, tiled=True)
    q1 = across(queries)
    q2 = partner(queries)
    q3 = across(q2)
    k_all = parts[:, 0].reshape(KEYS, HD)
    v_all = parts[:, 1].reshape(KEYS, HD)

    smem = pl.BlockSpec(memory_space=pltpu.SMEM)
    probs, stats = pl.pallas_call(
        score_kernel,
        out_shape=(
            jax.ShapeDtypeStruct((KEYS, ROWS), jnp.bfloat16),
            jax.ShapeDtypeStruct((2, ROWS), jnp.float32),
        ),
        in_specs=[smem, smem] + vmem(5),
        out_specs=tuple(vmem(2)),
        scratch_shapes=[pltpu.VMEM((KEYS, ROWS), jnp.float32), pltpu.VMEM((ROWS, HD), jnp.bfloat16)],
        compiler_params=pltpu.CompilerParams(vmem_limit_bytes=40 * MIB),
        name="scores",
    )(place, doc_lengths, k_all, queries, q1, q2, q3)

    s1 = across(stats)
    s2 = partner(stats)
    s3 = partner(stats, 13)
    cols, weight = pl.pallas_call(
        column_kernel,
        out_shape=(
            jax.ShapeDtypeStruct((NY * NX * NZL, PER), jnp.float32),
            jax.ShapeDtypeStruct((1, ROWS), jnp.float32),
        ),
        in_specs=vmem(5),
        out_specs=tuple(vmem(2)),
        compiler_params=pltpu.CompilerParams(vmem_limit_bytes=24 * MIB),
        name="columns",
    )(probs, stats, s1, s2, s3)

    got = lax.all_to_all(cols.reshape(NY * NX * NZL, 1, PER), ("y", "x", "zl"), 0, 0, tiled=True)
    totals = jnp.sum(got.reshape(NY * NX * NZL, NZL, CHUNK), axis=0) / HEADS
    scores = lax.dynamic_index_in_dim(totals, lax.axis_index("zl"), 0, keepdims=False)

    keep, send = pl.pallas_call(
        value_kernel,
        out_shape=(jax.ShapeDtypeStruct((2, HD, TOK), jnp.float32),) * 2,
        in_specs=vmem(3),
        out_specs=tuple(vmem(2)),
        compiler_params=pltpu.CompilerParams(vmem_limit_bytes=24 * MIB),
        name="rows",
    )(probs, v_all, weight)
    half = keep + across(send)
    rows = (half[0] + partner(half[1])).T.astype(jnp.bfloat16)
    return rows, scores


def solution(mesh):
    fine = Mesh(mesh.devices.reshape(NY, NZH, NX, NZL, NC), ("y", "zh", "x", "zl", "c"))
    ctx, head = ("y", "zh", "x"), ("zl", "c")
    return jax.shard_map(
        body,
        mesh=fine,
        in_specs=(P(ctx, head), P(ctx, None), P(ctx, None), P()),
        out_specs=(P(ctx, head), P(ctx + head)),
        check_vma=False,
    )
```

```python
import math

import jax
import jax.numpy as jnp
from jax import lax
from jax.experimental import pallas as pl
from jax.experimental.pallas import tpu as pltpu
from jax.sharding import Mesh, PartitionSpec as P

HD = 128
HEADS = 8
NY, NZH, NX, NZL, NC = 4, 2, 4, 4, 2
TOK = 256
CHUNK = TOK // HEADS
HALF = TOK // NC
BLOCKS = NY * NX
SIDE = BLOCKS * HALF
KEYS = NC * SIDE
ROWS = 2 * TOK
TILE = 512
SCALE = math.log2(math.e) / math.sqrt(HD)
MIB = 1024 * 1024
VMEM = pl.BlockSpec(memory_space=pltpu.VMEM)
SMEM = pl.BlockSpec(memory_space=pltpu.SMEM)


def spread_kernel(place_ref, keys_ref, values_ref, out_ref):
    half = pl.ds(pl.multiple_of(place_ref[3] * HALF, HALF), HALF)
    k, v = keys_ref[half, :], values_ref[half, :]
    for i in range(BLOCKS):
        out_ref[i, 0] = k
        out_ref[i, 1] = v


def score_kernel(place_ref, docs_ref, near_ref, far_ref, own_ref, other_ref, probs_ref, stats_ref, raw_ref):
    y, zh, x, c = place_ref[0], place_ref[1], place_ref[2], place_ref[3]
    e0 = docs_ref[0]
    e1 = e0 + docs_ref[1]
    e2 = e1 + docs_ref[2]
    own = (y * 8 + zh * 4 + x) * TOK
    other = (y * 8 + (1 - zh) * 4 + x) * TOK
    row = lax.broadcasted_iota(jnp.int32, (ROWS, 128), 0)
    pos = jnp.where(row < TOK, own, other) + lax.rem(row, TOK)
    start = jnp.zeros_like(pos)
    for end in (e0, e1, e2):
        start = jnp.where(pos >= end, end, start)
    lane = lax.broadcasted_iota(jnp.int32, (1, HALF), 1)
    queries = jnp.concatenate([own_ref[...], other_ref[...]], axis=0)

    peak = jnp.full((ROWS, 128), -1e30, jnp.float32)
    per = TILE // HALF
    for t in range(KEYS // TILE):
        ref, half = (near_ref, c) if t * TILE < SIDE else (far_ref, 1 - c)
        first = t * per % BLOCKS
        block = ref[pl.ds(first, per), 0].reshape(TILE, HD)
        raw = lax.dot_general(queries, block, (((1,), (1,)), ((), ())), preferred_element_type=jnp.float32)
        for j in range(per):
            source = first + j
            key_pos = (source // NX * 8 + zh * 4 + source % NX) * TOK + half * HALF + lane
            part = raw[:, j * HALF : (j + 1) * HALF]
            part = jnp.where((key_pos >= start) & (key_pos <= pos), part, -jnp.inf)
            raw_ref[:, t * TILE + j * HALF : t * TILE + (j + 1) * HALF] = part
            peak = jnp.maximum(peak, part)
    row_max = jnp.max(peak, axis=1, keepdims=True)

    total = jnp.zeros((ROWS, 128), jnp.float32)
    for j in range(KEYS // HALF):
        cut = slice(j * HALF, (j + 1) * HALF)
        probs = jnp.exp2((raw_ref[:, cut] - row_max) * SCALE)
        probs_ref[:, cut] = probs.astype(jnp.bfloat16)
        total = total + probs
    row_sum = jnp.sum(total, axis=1, keepdims=True)
    first_lane = lax.broadcasted_iota(jnp.int32, (ROWS, 128), 1) == 0
    stats_ref[...] = jnp.where(first_lane, row_max, row_sum).T[0:2, :]


def value_kernel(probs_ref, near_ref, far_ref, keep_ref, send_ref):
    acc = jnp.dot(probs_ref[:, :SIDE], near_ref[:, 1].reshape(SIDE, HD), preferred_element_type=jnp.float32)
    acc += jnp.dot(probs_ref[:, SIDE:], far_ref[:, 1].reshape(SIDE, HD), preferred_element_type=jnp.float32)
    keep_ref[...] = acc[:TOK]
    send_ref[...] = acc[TOK:].astype(jnp.bfloat16)


def shares(mine_ref, theirs_ref):
    both = theirs_ref[...]
    both = jnp.concatenate([both[:, TOK:], both[:, :TOK]], axis=1)
    m0, l0, m1, l1 = mine_ref[0:1, :], mine_ref[1:2, :], both[0:1, :], both[1:2, :]
    top = jnp.maximum(m0, m1)
    w0, w1 = jnp.exp2((m0 - top) * SCALE), jnp.exp2((m1 - top) * SCALE)
    norm = w0 * l0 + w1 * l1
    return w0 / norm, w1 / norm


def column_kernel(place_ref, probs_ref, mine_ref, theirs_ref, cols_ref):
    weight, _ = shares(mine_ref, theirs_ref)
    high = weight.astype(jnp.bfloat16).astype(jnp.float32)
    row = lax.broadcasted_iota(jnp.int32, (8, ROWS), 0)
    both = jnp.where(row == 0, high, jnp.where(row == 1, weight - high, 0.0)).astype(jnp.bfloat16)
    straight = place_ref[3] == 0

    def line(first):
        sums = jnp.dot(both, probs_ref[:, first : first + 2 * HALF], preferred_element_type=jnp.float32)
        return jnp.sum(sums, axis=0, keepdims=True)

    for b in range(0, BLOCKS, 2):
        near, far = line(b * HALF), line(SIDE + b * HALF)
        low, top = jnp.where(straight, near, far), jnp.where(straight, far, near)
        for i in range(2):
            cut = slice(i * HALF, (i + 1) * HALF)
            cols_ref[(b + i) * 8 : (b + i) * 8 + 4, :] = jnp.broadcast_to(low[:, cut], (4, HALF))
            cols_ref[(b + i) * 8 + 4 : (b + i) * 8 + 8, :] = jnp.broadcast_to(top[:, cut], (4, HALF))


def merge_kernel(keep_ref, got_ref, mine_ref, theirs_ref, out_ref):
    w0, w1 = shares(mine_ref, theirs_ref)
    w0 = jnp.broadcast_to(w0[:, :TOK], (HD, TOK)).T
    w1 = jnp.broadcast_to(w1[:, :TOK], (HD, TOK)).T
    out_ref[...] = (keep_ref[...] * w0 + got_ref[...].astype(jnp.float32) * w1).astype(jnp.bfloat16)


def kernel(fn, name, shapes, specs, scratch=(), limit=24):
    return pl.pallas_call(
        fn,
        out_shape=shapes,
        in_specs=specs,
        out_specs=jax.tree.map(lambda _: VMEM, shapes),
        scratch_shapes=scratch,
        compiler_params=pltpu.CompilerParams(vmem_limit_bytes=limit * MIB),
        name=name,
    )


def body(queries, keys, values, doc_lengths):
    shape = jax.ShapeDtypeStruct
    f32, bf16 = jnp.float32, jnp.bfloat16
    place = jnp.stack([lax.axis_index(a) for a in ("y", "zh", "x", "c")]).astype(jnp.int32)

    def across(x):
        return lax.ppermute(x, "c", [(0, 1), (1, 0)])

    def partner(x):
        return lax.ppermute(x, ("zh", "zl", "c"), [(i, i ^ 12) for i in range(16)])

    copies = kernel(spread_kernel, "spread", shape((BLOCKS, 2, HALF, HD), bf16), [SMEM, VMEM, VMEM])(
        place, keys, values
    )
    other = partner(queries)
    near = lax.all_to_all(copies, ("y", "x"), 0, 0, tiled=True)
    far = across(near)
    probs, mine = kernel(
        score_kernel,
        "scores",
        (shape((ROWS, KEYS), bf16), shape((2, ROWS), f32)),
        [SMEM, SMEM, VMEM, VMEM, VMEM, VMEM],
        [pltpu.VMEM((ROWS, KEYS), f32)],
        limit=32,
    )(place, doc_lengths, near, far, queries, other)
    theirs = partner(mine)
    keep, send = kernel(
        value_kernel, "rows", (shape((TOK, HD), f32), shape((TOK, HD), bf16)), [VMEM, VMEM, VMEM]
    )(probs, near, far)
    got = partner(send)
    cols = kernel(column_kernel, "columns", shape((BLOCKS * HEADS, HALF), f32), [SMEM, VMEM, VMEM, VMEM])(
        place, probs, mine, theirs
    )
    parts = lax.all_to_all(cols.reshape(BLOCKS * HEADS, 1, HALF), ("y", "x", "zl", "c"), 0, 0, tiled=True)
    rows = kernel(merge_kernel, "merge", shape((TOK, HD), bf16), [VMEM, VMEM, VMEM, VMEM])(keep, got, mine, theirs)
    totals = (jnp.sum(parts, axis=(0, 1)) / HEADS).reshape(HALF // CHUNK, CHUNK)
    piece = lax.rem(lax.axis_index("zl") * NC + lax.axis_index("c"), HALF // CHUNK)
    return rows, lax.dynamic_index_in_dim(totals, piece, 0, keepdims=False)


def solution(mesh):
    fine = Mesh(mesh.devices.reshape(NY, NZH, NX, NZL, NC), ("y", "zh", "x", "zl", "c"))
    ctx, head = ("y", "zh", "x"), ("zl", "c")
    return jax.shard_map(
        body,
        mesh=fine,
        in_specs=(P(ctx, head), P(ctx, None), P(ctx, None), P()),
        out_specs=(P(ctx, head), P(ctx + head)),
        check_vma=False,
    )
```

```python
import functools
import math

import jax
import jax.numpy as jnp
from jax import lax
from jax.experimental import pallas as pl
from jax.experimental.pallas import tpu as pltpu
from jax.sharding import Mesh, PartitionSpec as P

HD = 128
HEADS = 8
AXES = {"y": 4, "zh": 2, "x": 4, "u": 2, "s": 2, "c": 2}
NX = AXES["x"]
TOK = 256
CHUNK = TOK // HEADS
PART = 2 * CHUNK
BLOCKS = AXES["y"] * NX
SIDE = BLOCKS * PART
KEYS = 2 * SIDE
FLIPS = 4
ROWS = FLIPS * TOK
TILE = 512
LANES = 128
SCALE = math.log2(math.e) / math.sqrt(HD)
MIB = 1024 * 1024
VMEM = pl.BlockSpec(memory_space=pltpu.VMEM)
SMEM = pl.BlockSpec(memory_space=pltpu.SMEM)
ANY = pl.BlockSpec(memory_space=pl.ANY)


def spread_kernel(place_ref, keys_ref, values_ref, out_ref, k_ref, v_ref, sems):
    copies = [
        pltpu.make_async_copy(keys_ref, k_ref, sems.at[0]),
        pltpu.make_async_copy(values_ref, v_ref, sems.at[1]),
    ]
    for copy in copies:
        copy.start()
    s, c = place_ref[3], place_ref[4]
    for n, (copy, ref) in enumerate(zip(copies, (k_ref, v_ref))):
        copy.wait()
        for u in range(2):
            piece = ref[pl.ds(pl.multiple_of(((u * 2 + s) * 2 + c) * CHUNK, CHUNK), CHUNK), :]
            for i in range(BLOCKS):
                out_ref[i, n, u * CHUNK : (u + 1) * CHUNK] = piece


def score_kernel(place_ref, docs_ref, near_ref, far_ref, q0, q1, q2, q3, probs_ref, stats_ref, raw_ref):
    y, zh, x, s, c = (place_ref[i] for i in range(5))
    e0 = docs_ref[0]
    e1 = e0 + docs_ref[1]
    e2 = e1 + docs_ref[2]
    own = (y * 8 + zh * 4 + x) * TOK
    other = (y * 8 + (1 - zh) * 4 + x) * TOK
    row = lax.broadcasted_iota(jnp.int32, (ROWS, LANES), 0)
    pos = jnp.where(row < 2 * TOK, own, other) + lax.rem(row, TOK)
    start = jnp.zeros_like(pos)
    for end in (e0, e1, e2):
        start = jnp.where(pos >= end, end, start)
    lane = lax.broadcasted_iota(jnp.int32, (1, LANES), 1)
    queries = jnp.concatenate([q[...] for q in (q0, q1, q2, q3)], axis=0)

    peak = jnp.full((ROWS, LANES), -1e30, jnp.float32)
    per = TILE // PART
    for t in range(KEYS // TILE):
        ref, side = (near_ref, c) if t * TILE < SIDE else (far_ref, 1 - c)
        first = t * per % BLOCKS
        block = ref[pl.ds(first, per), 0].reshape(TILE, HD)
        raw = lax.dot_general(queries, block, (((1,), (1,)), ((), ())), preferred_element_type=jnp.float32)
        for j in range(TILE // LANES):
            source = first + j * (LANES // PART) + lane // PART
            key_pos = (
                (source // NX * 8 + zh * 4 + source % NX) * TOK
                + ((lane % PART // CHUNK * 2 + s) * 2 + side) * CHUNK
                + lane % CHUNK
            )
            part = raw[:, j * LANES : (j + 1) * LANES]
            part = jnp.where((key_pos >= start) & (key_pos <= pos), part, -jnp.inf)
            raw_ref[:, t * TILE + j * LANES : t * TILE + (j + 1) * LANES] = part
            peak = jnp.maximum(peak, part)
    row_max = jnp.max(peak, axis=1, keepdims=True)

    total = jnp.zeros((ROWS, LANES), jnp.float32)
    for j in range(KEYS // LANES):
        cut = slice(j * LANES, (j + 1) * LANES)
        probs = jnp.exp2((raw_ref[:, cut] - row_max) * SCALE)
        probs_ref[:, cut] = probs.astype(jnp.bfloat16)
        total = total + probs
    row_sum = jnp.sum(total, axis=1, keepdims=True)
    first_lane = lax.broadcasted_iota(jnp.int32, (ROWS, LANES), 1) == 0
    stats_ref[...] = jnp.where(first_lane, row_max, row_sum).T[0:2, :]


def value_kernel(probs_ref, near_ref, far_ref, keep_ref, a_ref, b_ref, ab_ref):
    acc = jnp.dot(probs_ref[:, :SIDE], near_ref[:, 1].reshape(SIDE, HD), preferred_element_type=jnp.float32)
    acc += jnp.dot(probs_ref[:, SIDE:], far_ref[:, 1].reshape(SIDE, HD), preferred_element_type=jnp.float32)
    keep_ref[...] = acc[:TOK]
    for k, ref in enumerate((a_ref, b_ref, ab_ref)):
        ref[...] = acc[(k + 1) * TOK : (k + 2) * TOK].astype(jnp.bfloat16)


def shares(refs):
    parts = []
    for flip, ref in enumerate(refs):
        both = jnp.concatenate([ref[:, (k ^ flip) * TOK : ((k ^ flip) + 1) * TOK] for k in range(FLIPS)], axis=1)
        parts.append((both[0:1, :], both[1:2, :]))
    top = functools.reduce(jnp.maximum, [m for m, _ in parts])
    weights = [jnp.exp2((m - top) * SCALE) for m, _ in parts]
    norm = sum(w * l for w, (_, l) in zip(weights, parts))
    return [w / norm for w in weights]


def column_kernel(place_ref, probs_ref, s0, s1, s2, s3, a_ref, cols_ref):
    weight = shares((s0, s1, s2, s3))[0]
    high = weight.astype(jnp.bfloat16).astype(jnp.float32)
    row = lax.broadcasted_iota(jnp.int32, (8, ROWS), 0)
    both = jnp.where(row == 0, high, jnp.where(row == 1, weight - high, 0.0)).astype(jnp.bfloat16)
    straight = place_ref[4] == 0

    def line(first):
        sums = jnp.dot(both, probs_ref[:, first : first + 2 * LANES], preferred_element_type=jnp.float32)
        return jnp.sum(sums, axis=0, keepdims=True)

    row8 = lax.broadcasted_iota(jnp.int32, (8, LANES), 0)
    for b in range(0, SIDE // LANES, 2):
        near, far = line(b * LANES), line(SIDE + b * LANES)
        even, odd = jnp.where(straight, near, far), jnp.where(straight, far, near)
        for i in range(2):
            cut = slice(i * LANES, (i + 1) * LANES)
            cols_ref[(b + i) * 8 : (b + i + 1) * 8, :] = jnp.where(row8 % 2 == 0, even[:, cut], odd[:, cut])


def merge_kernel(keep_ref, a_ref, b_ref, ab_ref, s0, s1, s2, s3, out_ref):
    weights = shares((s0, s1, s2, s3))
    out = jnp.zeros((TOK, HD), jnp.float32)
    for w, ref in zip(weights, (keep_ref, a_ref, b_ref, ab_ref)):
        out += ref[...].astype(jnp.float32) * jnp.broadcast_to(w[:, :TOK], (HD, TOK)).T
    out_ref[...] = out.astype(jnp.bfloat16)


def kernel(fn, name, shapes, specs, scratch=(), limit=24):
    return pl.pallas_call(
        fn,
        out_shape=shapes,
        in_specs=specs,
        out_specs=jax.tree.map(lambda _: VMEM, shapes),
        scratch_shapes=scratch,
        compiler_params=pltpu.CompilerParams(vmem_limit_bytes=limit * MIB),
        name=name,
    )


def body(queries, keys, values, doc_lengths):
    shape = jax.ShapeDtypeStruct
    f32, bf16 = jnp.float32, jnp.bfloat16
    place = jnp.stack([lax.axis_index(a) for a in ("y", "zh", "x", "s", "c")]).astype(jnp.int32)

    def across(x):
        return lax.ppermute(x, "c", [(0, 1), (1, 0)])

    def flipped(x, flip):
        mask = {1: 2, 2: 12, 3: 14}[flip]
        return lax.ppermute(x, ("zh", "u", "s", "c"), [(i, i ^ mask) for i in range(16)])

    copies = kernel(
        spread_kernel,
        "spread",
        shape((BLOCKS, 2, PART, HD), bf16),
        [SMEM, ANY, ANY],
        [pltpu.VMEM((TOK, HD), bf16), pltpu.VMEM((TOK, HD), bf16), pltpu.SemaphoreType.DMA((2,))],
    )(place, keys, values)
    others = [flipped(queries, k) for k in (1, 2, 3)]
    near = lax.all_to_all(copies, ("y", "x"), 0, 0, tiled=True)
    near, others = lax.optimization_barrier((near, others))
    far = across(near)
    probs, mine = kernel(
        score_kernel,
        "scores",
        (shape((ROWS, KEYS), bf16), shape((2, ROWS), f32)),
        [SMEM, SMEM] + [VMEM] * 6,
        [pltpu.VMEM((ROWS, KEYS), f32)],
        limit=32,
    )(place, doc_lengths, near, far, queries, *others)
    stats = [mine] + [flipped(mine, k) for k in (1, 2, 3)]
    keep, *send = kernel(
        value_kernel, "rows", (shape((TOK, HD), f32),) + (shape((TOK, HD), bf16),) * 3, [VMEM, VMEM, VMEM]
    )(probs, near, far)
    got = [flipped(piece, k + 1) for k, piece in enumerate(send)]
    cols = kernel(column_kernel, "columns", shape((BLOCKS * 4, LANES), f32), [SMEM] + [VMEM] * 5 + [ANY])(
        place, probs, *stats, send[0]
    )
    parts = lax.all_to_all(cols.reshape(BLOCKS * 4, 1, LANES), ("y", "x", "u", "c"), 0, 0, tiled=True)
    rows = kernel(merge_kernel, "merge", shape((TOK, HD), bf16), [VMEM] * 8)(keep, *got, *stats)
    totals = (jnp.sum(parts, axis=(0, 1)) / HEADS).reshape(LANES // CHUNK, CHUNK)
    piece = lax.rem(lax.axis_index("x"), 2) * 2 + lax.axis_index("u")
    return rows, lax.dynamic_index_in_dim(totals, piece, 0, keepdims=False)


def solution(mesh):
    fine = Mesh(mesh.devices.reshape(tuple(AXES.values())), tuple(AXES))
    ctx, head = ("y", "zh", "x"), ("u", "s", "c")
    return jax.shard_map(
        body,
        mesh=fine,
        in_specs=(P(ctx, head), P(ctx, None), P(ctx, None), P()),
        out_specs=(P(ctx, head), P(ctx + head)),
        check_vma=False,
    )
```

```python
import math

import jax
import jax.numpy as jnp
from jax import lax
from jax.experimental import pallas as pl
from jax.experimental.pallas import tpu as pltpu
from jax.sharding import Mesh, PartitionSpec as P

HD = 128
HEADS = 8
AXES = {"y": 4, "zh": 2, "x": 4, "zl": 4, "c": 2}
NX = AXES["x"]
TOK = 256
CHUNK = TOK // HEADS
HALF = TOK // 2
BLOCKS = AXES["y"] * NX
SIDE = BLOCKS * HALF
KEYS = 2 * SIDE
ROWS = 2 * TOK
TILE = 512
SCALE = math.log2(math.e) / math.sqrt(HD)
HEAD = 32
MIB = 1024 * 1024
VMEM = pl.BlockSpec(memory_space=pltpu.VMEM)
ANY = pl.BlockSpec(memory_space=pl.ANY)
SMEM = pl.BlockSpec(memory_space=pltpu.SMEM)


def my_half():
    return pl.ds(pl.multiple_of(lax.axis_index("c") * HALF, HALF), HALF)


def row_positions():
    y, zh, x = (lax.axis_index(a) for a in ("y", "zh", "x"))
    own = (y * 8 + zh * 4 + x) * TOK
    other = (y * 8 + (1 - zh) * 4 + x) * TOK
    row = lax.broadcasted_iota(jnp.int32, (ROWS, HALF), 0)
    return jnp.where(row < TOK, own, other) + lax.rem(row, TOK)


def spread_kernel(keys_ref, values_ref, out_ref, piece_ref, in_sems, out_sems):
    reads = [
        pltpu.make_async_copy(ref.at[my_half()], piece_ref.at[n], in_sems.at[n])
        for n, ref in enumerate((keys_ref, values_ref))
    ]
    for copy in reads:
        copy.start()
    for copy in reads:
        copy.wait()
    writes = [pltpu.make_async_copy(piece_ref, out_ref.at[i], out_sems.at[i]) for i in range(BLOCKS)]
    for copy in writes:
        copy.start()
    for copy in writes:
        copy.wait()


def limit_kernel(docs_ref, own_ref, q_ref, start_ref):
    q_ref[...] = own_ref[...]
    pos = row_positions()
    start = jnp.zeros_like(pos)
    end = 0
    for i in range(3):
        end = end + docs_ref[i]
        start = jnp.where(pos >= end, end, start)
    start_ref[...] = start


def masked_logits(keys_ref, half, own_ref, other_ref, start_ref, raw_ref):
    zh = lax.axis_index("zh")
    pos, start = row_positions(), start_ref[...]
    lane = lax.broadcasted_iota(jnp.int32, (1, HALF), 1)
    queries = jnp.concatenate([own_ref[...], other_ref[...]], axis=0)
    peak = jnp.full((ROWS, HALF), -1e30, jnp.float32)
    per = TILE // HALF
    for t in range(SIDE // TILE):
        block = keys_ref[pl.ds(t * per, per)].reshape(TILE, HD)
        raw = lax.dot_general(queries, block, (((1,), (1,)), ((), ())), preferred_element_type=jnp.float32)
        for j in range(per):
            source = t * per + j
            key_pos = (source // NX * 8 + zh * 4 + source % NX) * TOK + half * HALF + lane
            part = raw[:, j * HALF : (j + 1) * HALF]
            part = jnp.where((key_pos >= start) & (key_pos <= pos), part, -jnp.inf)
            raw_ref[:, source * HALF : (source + 1) * HALF] = part
            peak = jnp.maximum(peak, part)
    return peak


def near_kernel(near_ref, own_ref, other_ref, start_ref, raw_ref, peak_ref):
    peak_ref[...] = masked_logits(near_ref, lax.axis_index("c"), own_ref, other_ref, start_ref, raw_ref)


def score_kernel(
    k_ref, own_ref, other_ref, start_ref, near_raw_ref, peak_ref, near_ref, far_ref,
    probs_ref, stats_ref, keep_ref, send_ref, far_raw_ref,
):
    peak = masked_logits(k_ref, 1 - lax.axis_index("c"), own_ref, other_ref, start_ref, far_raw_ref)
    row_max = jnp.max(jnp.maximum(peak, peak_ref[...]), axis=1, keepdims=True)
    total = jnp.zeros((ROWS, HALF), jnp.float32)
    for side, raw_ref in enumerate((near_raw_ref, far_raw_ref)):
        for j in range(BLOCKS):
            probs = jnp.exp2((raw_ref[:, j * HALF : (j + 1) * HALF] - row_max) * SCALE)
            first = side * SIDE + j * HALF
            probs_ref[:, first : first + HALF] = probs.astype(jnp.bfloat16)
            total = total + probs
    acc = jnp.dot(probs_ref[:, :SIDE], near_ref[...].reshape(SIDE, HD), preferred_element_type=jnp.float32)
    acc += jnp.dot(probs_ref[:, SIDE:], far_ref[...].reshape(SIDE, HD), preferred_element_type=jnp.float32)
    row_sum = jnp.sum(total, axis=1, keepdims=True)
    first_lane = lax.broadcasted_iota(jnp.int32, (ROWS, HALF), 1) == 0
    stats = jnp.where(first_lane, row_max, row_sum).T[0:2, :]
    stats_ref[...] = stats
    pieces, rest = [], stats
    for _ in range(3):
        piece = rest.astype(jnp.bfloat16).astype(jnp.float32)
        pieces.append(piece)
        rest = rest - piece
    table = jnp.concatenate(pieces + [jnp.zeros_like(rest)], axis=0)
    table = jnp.concatenate([table[:, i * 128 : (i + 1) * 128] for i in range(ROWS // 128)], axis=0)
    keep_ref[...] = acc[:TOK]
    send_ref[0:HEAD, :] = table.astype(jnp.bfloat16)
    send_ref[HEAD:, :] = acc[TOK:].astype(jnp.bfloat16)


def shares(mine_ref, got_ref):
    table = got_ref[0:HEAD, :].astype(jnp.float32)
    rows = []
    for i in (2, 3, 0, 1):
        part = table[i * 8 : (i + 1) * 8]
        rows.append(part[0:2] + part[2:4] + part[4:6])
    both = jnp.concatenate(rows, axis=1)
    m0, l0, m1, l1 = mine_ref[0:1, :], mine_ref[1:2, :], both[0:1, :], both[1:2, :]
    top = jnp.maximum(m0, m1)
    w0, w1 = jnp.exp2((m0 - top) * SCALE), jnp.exp2((m1 - top) * SCALE)
    norm = w0 * l0 + w1 * l1
    return w0 / norm, w1 / norm


def column_kernel(probs_ref, mine_ref, got_ref, cols_ref):
    weight, _ = shares(mine_ref, got_ref)
    high = weight.astype(jnp.bfloat16).astype(jnp.float32)
    row = lax.broadcasted_iota(jnp.int32, (8, ROWS), 0)
    both = jnp.where(row == 0, high, jnp.where(row == 1, weight - high, 0.0)).astype(jnp.bfloat16)
    straight = lax.axis_index("c") == 0

    def line(first):
        sums = jnp.dot(both, probs_ref[:, first : first + 2 * HALF], preferred_element_type=jnp.float32)
        return jnp.sum(sums, axis=0, keepdims=True)

    row8 = lax.broadcasted_iota(jnp.int32, (8, HALF), 0)
    for b in range(0, BLOCKS, 2):
        near, far = line(b * HALF), line(SIDE + b * HALF)
        low, top = jnp.where(straight, near, far), jnp.where(straight, far, near)
        for i in range(2):
            cut = slice(i * HALF, (i + 1) * HALF)
            cols_ref[(b + i) * 8 : (b + i + 1) * 8, :] = jnp.where(row8 < 4, low[:, cut], top[:, cut])


def merge_kernel(keep_ref, got_ref, mine_ref, out_ref):
    w0, w1 = shares(mine_ref, got_ref)
    w0 = jnp.broadcast_to(w0[:, :TOK], (HD, TOK)).T
    w1 = jnp.broadcast_to(w1[:, :TOK], (HD, TOK)).T
    got = got_ref[HEAD:, :].astype(jnp.float32)
    out_ref[...] = (keep_ref[...] * w0 + got * w1).astype(jnp.bfloat16)


def kernel(fn, name, shapes, specs, scratch=(), limit=8, space=VMEM):
    return pl.pallas_call(
        fn,
        out_shape=shapes,
        in_specs=specs,
        out_specs=jax.tree.map(lambda _: space, shapes),
        scratch_shapes=scratch,
        compiler_params=pltpu.CompilerParams(vmem_limit_bytes=limit * MIB),
        name=name,
    )


def body(queries, keys, values, doc_lengths):
    shape = jax.ShapeDtypeStruct
    f32, bf16 = jnp.float32, jnp.bfloat16
    def across(x):
        return lax.ppermute(x, "c", [(0, 1), (1, 0)])

    def partner(x):
        return lax.ppermute(x, ("zh", "zl", "c"), [(i, i ^ 12) for i in range(16)])

    copies = kernel(
        spread_kernel,
        "spread",
        shape((BLOCKS, 2, HALF, HD), bf16),
        [ANY] * 2,
        [
            pltpu.VMEM((2, HALF, HD), bf16),
            pltpu.SemaphoreType.DMA((2,)),
            pltpu.SemaphoreType.DMA((BLOCKS,)),
        ],
        limit=60,
        space=ANY,
    )(keys, values)
    near = lax.all_to_all(copies, ("y", "x"), 0, 0, tiled=True)
    other = partner(queries)
    own, start = kernel(
        limit_kernel, "limits", (shape((TOK, HD), bf16), shape((ROWS, HALF), jnp.int32)), [SMEM, VMEM]
    )(doc_lengths, queries)
    near, other, own, start = lax.optimization_barrier((near, other, own, start))
    k_near, v_near = near[:, 0], near[:, 1]
    k_far, v_far = across(k_near), across(v_near)
    raw, peak = kernel(
        near_kernel, "near_scores", (shape((ROWS, SIDE), f32), shape((ROWS, HALF), f32)), [VMEM] * 4, limit=12
    )(k_near, own, other, start)
    probs, mine, keep, send = kernel(
        score_kernel,
        "scores",
        (
            shape((ROWS, KEYS), bf16),
            shape((2, ROWS), f32),
            shape((TOK, HD), f32),
            shape((HEAD + TOK, HD), bf16),
        ),
        [VMEM] * 8,
        [pltpu.VMEM((ROWS, SIDE), f32)],
        limit=20,
    )(k_far, own, other, start, raw, peak, v_near, v_far)
    got = partner(send)
    cols = kernel(column_kernel, "columns", shape((BLOCKS * HEADS, HALF), f32), [VMEM] * 3)(probs, mine, got)
    parts = lax.all_to_all(cols.reshape(BLOCKS * HEADS, 1, HALF), ("y", "x", "zl", "c"), 0, 0, tiled=True)
    rows = kernel(merge_kernel, "merge", shape((TOK, HD), bf16), [VMEM] * 3)(keep, got, mine)
    totals = (jnp.sum(parts, axis=(0, 1)) / HEADS).reshape(HALF // CHUNK, CHUNK)
    piece = lax.rem(lax.axis_index("zl") * 2 + lax.axis_index("c"), HALF // CHUNK)
    return rows, lax.dynamic_index_in_dim(totals, piece, 0, keepdims=False)


def solution(mesh):
    fine = Mesh(mesh.devices.reshape(tuple(AXES.values())), tuple(AXES))
    ctx, head = ("y", "zh", "x"), ("zl", "c")
    return jax.shard_map(
        body,
        mesh=fine,
        in_specs=(P(ctx, head), P(ctx, None), P(ctx, None), P()),
        out_specs=(P(ctx, head), P(ctx + head)),
        check_vma=False,
    )
```

```python
import math

import jax
import jax.numpy as jnp
from jax import lax
from jax.experimental import pallas as pl
from jax.experimental.pallas import tpu as pltpu
from jax.sharding import Mesh, PartitionSpec as P

HD = 128
HEADS = 8
AXES = {"y": 4, "zh": 2, "x": 4, "zl": 4, "c": 2}
NX = AXES["x"]
TOK = 256
CHUNK = TOK // HEADS
HALF = TOK // 2
BLOCKS = AXES["y"] * NX
SIDE = BLOCKS * HALF
KEYS = 2 * SIDE
ROWS = 2 * TOK
TILE = 512
SCALE = math.log2(math.e) / math.sqrt(HD)
LONG = 20_000_000_000
MIB = 1024 * 1024
VMEM = pl.BlockSpec(memory_space=pltpu.VMEM)
ANY = pl.BlockSpec(memory_space=pl.ANY)
SMEM = pl.BlockSpec(memory_space=pltpu.SMEM)


def my_half():
    return pl.ds(pl.multiple_of(lax.axis_index("c") * HALF, HALF), HALF)


def row_positions():
    y, zh, x = (lax.axis_index(a) for a in ("y", "zh", "x"))
    own = (y * 8 + zh * 4 + x) * TOK
    other = (y * 8 + (1 - zh) * 4 + x) * TOK
    row = lax.broadcasted_iota(jnp.int32, (ROWS, HALF), 0)
    return jnp.where(row < TOK, own, other) + lax.rem(row, TOK)


def spread_kernel(keys_ref, values_ref, out_ref, piece_ref, in_sems, out_sems):
    reads = [
        pltpu.make_async_copy(ref.at[my_half()], piece_ref.at[n], in_sems.at[n])
        for n, ref in enumerate((keys_ref, values_ref))
    ]
    for copy in reads:
        copy.start()
    for copy in reads:
        copy.wait()
    writes = [pltpu.make_async_copy(piece_ref, out_ref.at[i], out_sems.at[i]) for i in range(BLOCKS)]
    for copy in writes:
        copy.start()
    for copy in writes:
        copy.wait()


def limit_kernel(docs_ref, own_ref, q_ref, start_ref):
    q_ref[...] = own_ref[...]
    pos = row_positions()
    start = jnp.zeros_like(pos)
    end = 0
    for i in range(3):
        end = end + docs_ref[i]
        start = jnp.where(pos >= end, end, start)
    start_ref[...] = start


def masked_logits(keys_ref, half, own_ref, other_ref, start_ref, raw_ref):
    zh = lax.axis_index("zh")
    pos, start = row_positions(), start_ref[...]
    lane = lax.broadcasted_iota(jnp.int32, (1, HALF), 1)
    queries = jnp.concatenate([own_ref[...], other_ref[...]], axis=0)
    peak = jnp.full((ROWS, HALF), -1e30, jnp.float32)
    per = TILE // HALF
    for t in range(SIDE // TILE):
        block = keys_ref[pl.ds(t * per, per)].reshape(TILE, HD)
        raw = lax.dot_general(queries, block, (((1,), (1,)), ((), ())), preferred_element_type=jnp.float32)
        for j in range(per):
            source = t * per + j
            key_pos = (source // NX * 8 + zh * 4 + source % NX) * TOK + half * HALF + lane
            part = raw[:, j * HALF : (j + 1) * HALF]
            part = jnp.where((key_pos >= start) & (key_pos <= pos), part, -jnp.inf)
            raw_ref[:, source * HALF : (source + 1) * HALF] = part
            peak = jnp.maximum(peak, part)
    return peak


def near_kernel(near_ref, own_ref, other_ref, start_ref, raw_ref, peak_ref):
    peak_ref[...] = masked_logits(near_ref, lax.axis_index("c"), own_ref, other_ref, start_ref, raw_ref)


def score_kernel(
    k_ref, own_ref, other_ref, start_ref, near_raw_ref, peak_ref, probs_ref, stats_ref, far_raw_ref
):
    peak = masked_logits(k_ref, 1 - lax.axis_index("c"), own_ref, other_ref, start_ref, far_raw_ref)
    row_max = jnp.max(jnp.maximum(peak, peak_ref[...]), axis=1, keepdims=True)
    total = jnp.zeros((ROWS, HALF), jnp.float32)
    for side, raw_ref in enumerate((near_raw_ref, far_raw_ref)):
        for j in range(BLOCKS):
            probs = jnp.exp2((raw_ref[:, j * HALF : (j + 1) * HALF] - row_max) * SCALE)
            first = side * SIDE + j * HALF
            probs_ref[:, first : first + HALF] = probs.astype(jnp.bfloat16)
            total = total + probs
    row_sum = jnp.sum(total, axis=1, keepdims=True)
    first_lane = lax.broadcasted_iota(jnp.int32, (ROWS, HALF), 1) == 0
    stats_ref[...] = jnp.where(first_lane, row_max, row_sum).T[0:2, :]


def row_kernel(probs_ref, near_ref, far_ref, keep_ref, send_ref):
    acc = jnp.dot(probs_ref[:, :SIDE], near_ref[...].reshape(SIDE, HD), preferred_element_type=jnp.float32)
    acc += jnp.dot(probs_ref[:, SIDE:], far_ref[...].reshape(SIDE, HD), preferred_element_type=jnp.float32)
    keep_ref[...] = acc[:TOK]
    send_ref[...] = acc[TOK:].astype(jnp.bfloat16)


def shares(mine_ref, theirs_ref):
    both = theirs_ref[...]
    both = jnp.concatenate([both[:, TOK:], both[:, :TOK]], axis=1)
    m0, l0, m1, l1 = mine_ref[0:1, :], mine_ref[1:2, :], both[0:1, :], both[1:2, :]
    top = jnp.maximum(m0, m1)
    w0, w1 = jnp.exp2((m0 - top) * SCALE), jnp.exp2((m1 - top) * SCALE)
    norm = w0 * l0 + w1 * l1
    return w0 / norm, w1 / norm


def column_kernel(probs_ref, mine_ref, theirs_ref, cols_ref):
    weight, _ = shares(mine_ref, theirs_ref)
    high = weight.astype(jnp.bfloat16).astype(jnp.float32)
    row = lax.broadcasted_iota(jnp.int32, (8, ROWS), 0)
    both = jnp.where(row == 0, high, jnp.where(row == 1, weight - high, 0.0)).astype(jnp.bfloat16)
    straight = lax.axis_index("c") == 0

    def line(first):
        sums = jnp.dot(both, probs_ref[:, first : first + 2 * HALF], preferred_element_type=jnp.float32)
        return jnp.sum(sums, axis=0, keepdims=True)

    row8 = lax.broadcasted_iota(jnp.int32, (8, HALF), 0)
    for b in range(0, BLOCKS, 2):
        near, far = line(b * HALF), line(SIDE + b * HALF)
        low, top = jnp.where(straight, near, far), jnp.where(straight, far, near)
        for i in range(2):
            cut = slice(i * HALF, (i + 1) * HALF)
            cols_ref[(b + i) * 8 : (b + i + 1) * 8, :] = jnp.where(row8 < 4, low[:, cut], top[:, cut])


def merge_kernel(keep_ref, got_ref, mine_ref, theirs_ref, out_ref):
    w0, w1 = shares(mine_ref, theirs_ref)
    w0 = jnp.broadcast_to(w0[:, :TOK], (HD, TOK)).T
    w1 = jnp.broadcast_to(w1[:, :TOK], (HD, TOK)).T
    out_ref[...] = (keep_ref[...] * w0 + got_ref[...].astype(jnp.float32) * w1).astype(jnp.bfloat16)


def kernel(fn, name, shapes, specs, scratch=(), limit=8, space=VMEM, flops=0):
    return pl.pallas_call(
        fn,
        out_shape=shapes,
        in_specs=specs,
        out_specs=jax.tree.map(lambda _: space, shapes),
        scratch_shapes=scratch,
        compiler_params=pltpu.CompilerParams(vmem_limit_bytes=limit * MIB),
        cost_estimate=pl.CostEstimate(flops=flops, bytes_accessed=0, transcendentals=0) if flops else None,
        name=name,
    )


def body(queries, keys, values, doc_lengths):
    shape = jax.ShapeDtypeStruct
    f32, bf16 = jnp.float32, jnp.bfloat16
    def across(x):
        return lax.ppermute(x, "c", [(0, 1), (1, 0)])

    def partner(x):
        return lax.ppermute(x, ("zh", "zl", "c"), [(i, i ^ 12) for i in range(16)])

    copies = kernel(
        spread_kernel,
        "spread",
        shape((BLOCKS, 2, HALF, HD), bf16),
        [ANY] * 2,
        [
            pltpu.VMEM((2, HALF, HD), bf16),
            pltpu.SemaphoreType.DMA((2,)),
            pltpu.SemaphoreType.DMA((BLOCKS,)),
        ],
        limit=60,
        space=ANY,
    )(keys, values)
    near = lax.all_to_all(copies, ("y", "x"), 0, 0, tiled=True)
    other = partner(queries)
    own, start = kernel(
        limit_kernel, "limits", (shape((TOK, HD), bf16), shape((ROWS, HALF), jnp.int32)), [SMEM, VMEM]
    )(doc_lengths, queries)
    near, other, own, start = lax.optimization_barrier((near, other, own, start))
    k_near, v_near = near[:, 0], near[:, 1]
    k_far, v_far = across(k_near), across(v_near)
    raw, peak = kernel(
        near_kernel, "near_scores", (shape((ROWS, SIDE), f32), shape((ROWS, HALF), f32)), [VMEM] * 4, limit=12
    )(k_near, own, other, start)
    probs, mine = kernel(
        score_kernel,
        "scores",
        (shape((ROWS, KEYS), bf16), shape((2, ROWS), f32)),
        [VMEM] * 6,
        [pltpu.VMEM((ROWS, SIDE), f32)],
        limit=20,
    )(k_far, own, other, start, raw, peak)
    theirs = partner(mine)
    keep, send = kernel(
        row_kernel, "rows", (shape((TOK, HD), f32), shape((TOK, HD), bf16)), [VMEM] * 3, flops=LONG
    )(probs, v_near, v_far)
    got = partner(send)
    cols = kernel(
        column_kernel, "columns", shape((BLOCKS * HEADS, HALF), f32), [VMEM] * 3, flops=LONG
    )(probs, mine, theirs)
    parts = lax.all_to_all(cols.reshape(BLOCKS * HEADS, 1, HALF), ("y", "x", "zl", "c"), 0, 0, tiled=True)
    rows = kernel(merge_kernel, "merge", shape((TOK, HD), bf16), [VMEM] * 4, flops=LONG)(keep, got, mine, theirs)
    totals = (jnp.sum(parts, axis=(0, 1)) / HEADS).reshape(HALF // CHUNK, CHUNK)
    piece = lax.rem(lax.axis_index("zl") * 2 + lax.axis_index("c"), HALF // CHUNK)
    return rows, lax.dynamic_index_in_dim(totals, piece, 0, keepdims=False)


def solution(mesh):
    fine = Mesh(mesh.devices.reshape(tuple(AXES.values())), tuple(AXES))
    ctx, head = ("y", "zh", "x"), ("zl", "c")
    return jax.shard_map(
        body,
        mesh=fine,
        in_specs=(P(ctx, head), P(ctx, None), P(ctx, None), P()),
        out_specs=(P(ctx, head), P(ctx + head)),
        check_vma=False,
    )
```

```python
import math

import jax
import jax.numpy as jnp
from jax import lax
from jax.experimental import pallas as pl
from jax.experimental.pallas import tpu as pltpu
from jax.sharding import Mesh, PartitionSpec as P

HD = 128
HEADS = 8
AXES = {"y": 4, "zh": 2, "x": 4, "zl": 4, "c": 2}
NX = AXES["x"]
NZL = AXES["zl"]
TOK = 256
CHUNK = TOK // HEADS
HALF = TOK // 2
BLOCKS = AXES["y"] * NX
KEYS = BLOCKS * HALF
FLIPS = 4
ROWS = FLIPS * TOK
TILE = 512
SCALE = math.log2(math.e) / math.sqrt(HD)
LONG = 20_000_000_000
MIB = 1024 * 1024
VMEM = pl.BlockSpec(memory_space=pltpu.VMEM)
ANY = pl.BlockSpec(memory_space=pl.ANY)
SMEM = pl.BlockSpec(memory_space=pltpu.SMEM)


def spread_kernel(keys_ref, values_ref, out_ref, piece_ref, in_sems, out_sems):
    c = lax.axis_index("c")
    reads = []
    for n, ref in enumerate((keys_ref, values_ref)):
        for z in range(NZL):
            rows = pl.ds(pl.multiple_of((z * 2 + c) * CHUNK, CHUNK), CHUNK)
            target = piece_ref.at[n, pl.ds(z * CHUNK, CHUNK)]
            reads.append(pltpu.make_async_copy(ref.at[rows], target, in_sems.at[n, z]))
    for copy in reads:
        copy.start()
    for copy in reads:
        copy.wait()
    writes = [pltpu.make_async_copy(piece_ref, out_ref.at[i], out_sems.at[i]) for i in range(BLOCKS)]
    for copy in writes:
        copy.start()
    for copy in writes:
        copy.wait()


def row_positions():
    y, zh, x = (lax.axis_index(a) for a in ("y", "zh", "x"))
    own = (y * 8 + zh * 4 + x) * TOK
    other = (y * 8 + (1 - zh) * 4 + x) * TOK
    row = lax.broadcasted_iota(jnp.int32, (ROWS, HALF), 0)
    return jnp.where(row < 2 * TOK, own, other) + lax.rem(row, TOK)


def limit_kernel(docs_ref, own_ref, q_ref, start_ref):
    q_ref[...] = own_ref[...]
    pos = row_positions()
    start = jnp.zeros_like(pos)
    end = 0
    for i in range(3):
        end = end + docs_ref[i]
        start = jnp.where(pos >= end, end, start)
    start_ref[...] = start


def score_kernel(near_ref, q0, q1, q2, q3, start_ref, probs_ref, stats_ref, raw_ref):
    zh, c = lax.axis_index("zh"), lax.axis_index("c")
    pos, start = row_positions(), start_ref[...]
    lane = lax.broadcasted_iota(jnp.int32, (1, HALF), 1)
    inside = (lane // CHUNK * 2 + c) * CHUNK + lane % CHUNK
    queries = jnp.concatenate([q[...] for q in (q0, q1, q2, q3)], axis=0)
    peak = jnp.full((ROWS, HALF), -1e30, jnp.float32)
    per = TILE // HALF
    for t in range(KEYS // TILE):
        block = near_ref[t * per : (t + 1) * per, 0].reshape(TILE, HD)
        raw = lax.dot_general(queries, block, (((1,), (1,)), ((), ())), preferred_element_type=jnp.float32)
        for j in range(per):
            source = t * per + j
            key_pos = (source // NX * 8 + zh * 4 + source % NX) * TOK + inside
            part = raw[:, j * HALF : (j + 1) * HALF]
            part = jnp.where((key_pos >= start) & (key_pos <= pos), part, -jnp.inf)
            raw_ref[:, source * HALF : (source + 1) * HALF] = part
            peak = jnp.maximum(peak, part)
    row_max = jnp.max(peak, axis=1, keepdims=True)
    total = jnp.zeros((ROWS, HALF), jnp.float32)
    for j in range(0, KEYS, HALF):
        probs = jnp.exp2((raw_ref[:, j : j + HALF] - row_max) * SCALE)
        probs_ref[:, j : j + HALF] = probs.astype(jnp.bfloat16)
        total = total + probs
    row_sum = jnp.sum(total, axis=1, keepdims=True)
    first_lane = lax.broadcasted_iota(jnp.int32, (ROWS, HALF), 1) == 0
    stats_ref[...] = jnp.where(first_lane, row_max, row_sum).T[0:2, :]


def row_kernel(probs_ref, near_ref, keep_ref, send_ref):
    acc = jnp.dot(probs_ref[...], near_ref[:, 1].reshape(KEYS, HD), preferred_element_type=jnp.float32)
    for k in range(2):
        keep_ref[k] = acc[2 * k * TOK : (2 * k + 1) * TOK]
        send_ref[k] = acc[(2 * k + 1) * TOK : (2 * k + 2) * TOK]


def stat(ref, k):
    cut = slice(k * TOK, (k + 1) * TOK)
    return ref[0:1, cut], ref[1:2, cut]


def as_column(row):
    return jnp.broadcast_to(row, (HD, TOK)).T


def pair_kernel(mine_ref, core_ref, send_ref, pair_ref):
    for k in range(FLIPS):
        (m0, l0), (m1, l1) = stat(mine_ref, k), stat(core_ref, k ^ 1)
        top = jnp.maximum(m0, m1)
        cut = slice(k * TOK, (k + 1) * TOK)
        pair_ref[0:1, cut] = top
        pair_ref[1:2, cut] = l0 * jnp.exp2((m0 - top) * SCALE) + l1 * jnp.exp2((m1 - top) * SCALE)


def join_kernel(keep_ref, got_ref, mine_ref, core_ref, keep_out_ref, send_ref):
    for k, ref in ((0, keep_out_ref), (2, send_ref)):
        m0, m1 = stat(mine_ref, k)[0], stat(core_ref, k ^ 1)[0]
        top = jnp.maximum(m0, m1)
        w0, w1 = jnp.exp2((m0 - top) * SCALE), jnp.exp2((m1 - top) * SCALE)
        joined = keep_ref[k // 2] * as_column(w0) + got_ref[k // 2] * as_column(w1)
        ref[...] = joined.astype(ref.dtype)


def column_kernel(probs_ref, mine_ref, pair_ref, plane_ref, send_ref, cols_ref):
    weight = []
    for k in range(FLIPS):
        (m0, l0), (m1, l1) = stat(pair_ref, k), stat(plane_ref, k ^ 2)
        top = jnp.maximum(m0, m1)
        norm = l0 * jnp.exp2((m0 - top) * SCALE) + l1 * jnp.exp2((m1 - top) * SCALE)
        weight.append(jnp.exp2((stat(mine_ref, k)[0] - top) * SCALE) / norm)
    weight = jnp.concatenate(weight, axis=1)
    high = weight.astype(jnp.bfloat16).astype(jnp.float32)
    row = lax.broadcasted_iota(jnp.int32, (8, ROWS), 0)
    both = jnp.where(row == 0, high, jnp.where(row == 1, weight - high, 0.0)).astype(jnp.bfloat16)
    for b in range(0, BLOCKS, 2):
        first = b * HALF
        sums = jnp.dot(both, probs_ref[:, first : first + 2 * HALF], preferred_element_type=jnp.float32)
        line = jnp.sum(sums, axis=0, keepdims=True)
        pair = [jnp.broadcast_to(line[:, i * HALF : (i + 1) * HALF], (NZL, HALF)) for i in range(2)]
        cols_ref[b * NZL : (b + 2) * NZL, :] = jnp.concatenate(pair, axis=0)


def merge_kernel(keep_ref, got_ref, pair_ref, plane_ref, out_ref):
    (m0, l0), (m1, l1) = stat(pair_ref, 0), stat(plane_ref, 2)
    top = jnp.maximum(m0, m1)
    w0, w1 = jnp.exp2((m0 - top) * SCALE), jnp.exp2((m1 - top) * SCALE)
    norm = w0 * l0 + w1 * l1
    out = keep_ref[...] * as_column(w0 / norm) + got_ref[...].astype(jnp.float32) * as_column(w1 / norm)
    out_ref[...] = out.astype(jnp.bfloat16)


def kernel(fn, name, shapes, specs, scratch=(), limit=8, space=VMEM, flops=0):
    return pl.pallas_call(
        fn,
        out_shape=shapes,
        in_specs=specs,
        out_specs=jax.tree.map(lambda _: space, shapes),
        scratch_shapes=scratch,
        compiler_params=pltpu.CompilerParams(vmem_limit_bytes=limit * MIB),
        cost_estimate=pl.CostEstimate(flops=flops, bytes_accessed=0, transcendentals=0) if flops else None,
        name=name,
    )


def body(queries, keys, values, doc_lengths):
    shape = jax.ShapeDtypeStruct
    f32, bf16 = jnp.float32, jnp.bfloat16
    def across(x):
        return lax.ppermute(x, "c", [(0, 1), (1, 0)])

    def partner(x):
        return lax.ppermute(x, ("zh", "zl", "c"), [(i, i ^ 12) for i in range(16)])

    copies = kernel(
        spread_kernel,
        "spread",
        shape((BLOCKS, 2, HALF, HD), bf16),
        [ANY] * 2,
        [
            pltpu.VMEM((2, HALF, HD), bf16),
            pltpu.SemaphoreType.DMA((2, NZL)),
            pltpu.SemaphoreType.DMA((BLOCKS,)),
        ],
        limit=60,
        space=ANY,
    )(keys, values)
    near = lax.all_to_all(copies, ("y", "x"), 0, 0, tiled=True)
    q1, q2 = across(queries), partner(queries)
    q3 = across(q2)
    own, start = kernel(
        limit_kernel, "limits", (shape((TOK, HD), bf16), shape((ROWS, HALF), jnp.int32)), [SMEM, VMEM]
    )(doc_lengths, queries)
    near, q1, q2, q3, own, start = lax.optimization_barrier((near, q1, q2, q3, own, start))
    probs, mine = kernel(
        score_kernel,
        "scores",
        (shape((ROWS, KEYS), bf16), shape((2, ROWS), f32)),
        [VMEM] * 6,
        [pltpu.VMEM((ROWS, KEYS), f32)],
        limit=24,
    )(near, own, q1, q2, q3, start)
    core = across(mine)
    keep, send = kernel(row_kernel, "rows", (shape((2, TOK, HD), f32),) * 2, [VMEM] * 2, flops=LONG)(probs, near)
    pair = kernel(pair_kernel, "pair", shape((2, ROWS), f32), [VMEM] * 2 + [ANY], flops=LONG)(mine, core, send)
    plane = partner(pair)
    keep, send = kernel(
        join_kernel, "join", (shape((TOK, HD), f32), shape((TOK, HD), bf16)), [VMEM] * 4, flops=LONG
    )(keep, across(send), mine, core)
    got = partner(send)
    cols = kernel(
        column_kernel, "columns", shape((BLOCKS * NZL, HALF), f32), [VMEM] * 4 + [ANY], flops=LONG
    )(probs, mine, pair, plane, send)
    parts = lax.all_to_all(cols.reshape(BLOCKS * NZL, 1, HALF), ("y", "x", "zl"), 0, 0, tiled=True)
    rows = kernel(merge_kernel, "merge", shape((TOK, HD), bf16), [VMEM] * 4, flops=LONG)(keep, got, pair, plane)
    parts, _ = lax.optimization_barrier((parts, rows))
    totals = (jnp.sum(parts, axis=(0, 1)) / HEADS).reshape(NZL, CHUNK)
    return rows, lax.dynamic_index_in_dim(totals, lax.axis_index("zl"), 0, keepdims=False)


def solution(mesh):
    fine = Mesh(mesh.devices.reshape(tuple(AXES.values())), tuple(AXES))
    ctx, head = ("y", "zh", "x"), ("zl", "c")
    return jax.shard_map(
        body,
        mesh=fine,
        in_specs=(P(ctx, head), P(ctx, None), P(ctx, None), P()),
        out_specs=(P(ctx, head), P(ctx + head)),
        check_vma=False,
    )
```

```python
import math

import jax
import jax.numpy as jnp
from jax import lax
from jax.experimental import pallas as pl
from jax.experimental.pallas import tpu as pltpu
from jax.sharding import Mesh, PartitionSpec as P

HD = 128
HEADS = 8
AXES = {"y": 4, "zh": 2, "x": 4, "zl": 4, "c": 2}
NX = AXES["x"]
NZL = AXES["zl"]
TOK = 256
CHUNK = TOK // HEADS
HALF = TOK // 2
BLOCKS = AXES["y"] * NX
KEYS = BLOCKS * HALF
FLIPS = 4
ROWS = FLIPS * TOK
TILE = 512
SCALE = math.log2(math.e) / math.sqrt(HD)
OWN, OTHER = 4, 5
BARRED = 32768.0
LONG = 20_000_000_000
MIB = 1024 * 1024
VMEM = pl.BlockSpec(memory_space=pltpu.VMEM)
ANY = pl.BlockSpec(memory_space=pl.ANY)
SMEM = pl.BlockSpec(memory_space=pltpu.SMEM)


def spread_kernel(keys_ref, values_ref, out_ref, piece_ref, in_sems, out_sems):
    c = lax.axis_index("c")
    reads = [
        pltpu.make_async_copy(ref.at[:, c], piece_ref.at[n], in_sems.at[n])
        for n, ref in enumerate((keys_ref, values_ref))
    ]
    for copy in reads:
        copy.start()
    for copy in reads:
        copy.wait()
    writes = [pltpu.make_async_copy(piece_ref, out_ref.at[i], out_sems.at[i]) for i in range(BLOCKS)]
    for copy in writes:
        copy.start()
    for copy in writes:
        copy.wait()


def inside_block(index):
    return (index // CHUNK * 2 + lax.axis_index("c")) * CHUNK + index % CHUNK


def limit_kernel(docs_ref, own_ref, q_ref, row_mask_ref, key_mask_ref):
    q_ref[...] = own_ref[...]
    y, zh, x = (lax.axis_index(a) for a in ("y", "zh", "x"))
    own, other = y * 8 + zh * 4 + x, y * 8 + (1 - zh) * 4 + x
    ends = [docs_ref[0]]
    for i in (1, 2):
        ends.append(ends[-1] + docs_ref[i])

    def document(pos):
        return sum((pos >= end).astype(jnp.int32) for end in ends)

    row = lax.broadcasted_iota(jnp.int32, (ROWS, HD), 0)
    lane = lax.broadcasted_iota(jnp.int32, (ROWS, HD), 1)
    mine = row < 2 * TOK
    doc = document(jnp.where(mine, own, other) * TOK + row % TOK)
    hit = (lane == doc) | (lane == jnp.where(mine, OWN, OTHER))
    row_mask_ref[...] = jnp.where(hit, 1.0, 0.0).astype(jnp.bfloat16)

    key = lax.broadcasted_iota(jnp.int32, (KEYS, HD), 0)
    lane = lax.broadcasted_iota(jnp.int32, (KEYS, HD), 1)
    slot = key // HALF
    block = slot // NX * 8 + zh * 4 + slot % NX
    doc = document(block * TOK + inside_block(key % HALF))
    barred = (lane < OWN) & (lane != doc)
    barred = barred | ((lane == OWN) & (block >= own)) | ((lane == OTHER) & (block > other))
    key_mask_ref[...] = jnp.where(barred, -BARRED, 0.0).astype(jnp.bfloat16)


def score_kernel(near_ref, q0, q1, q2, q3, row_mask_ref, key_mask_ref, probs_ref, stats_ref, raw_ref):
    across_depth = (((1,), (1,)), ((), ()))
    queries = jnp.concatenate([q[...] for q in (q0, q1, q2, q3)], axis=0)
    queries = jnp.concatenate([queries, row_mask_ref[...]], axis=1)
    own = 2 * TOK
    slot = lax.axis_index("y") * NX + lax.axis_index("x")
    mask = key_mask_ref[pl.ds(pl.multiple_of(slot * HALF, HALF), HALF), :]
    feature = lax.broadcasted_iota(jnp.int32, (HALF, HD), 1)
    mask = jnp.where(feature == OWN, 0.0, mask.astype(jnp.float32)).astype(jnp.bfloat16)
    block = jnp.concatenate([near_ref[slot, 0], mask], axis=1)
    diagonal = lax.dot_general(queries[:own], block, across_depth, preferred_element_type=jnp.float32)
    row = lax.broadcasted_iota(jnp.int32, (own, HALF), 0) % TOK
    lane = lax.broadcasted_iota(jnp.int32, (own, HALF), 1)
    diagonal = jnp.where(inside_block(lane) <= row, diagonal, -jnp.inf)
    peak = jnp.maximum(jnp.full((own, HALF), -1e30, jnp.float32), diagonal)
    peak = jnp.concatenate([peak, jnp.full((ROWS - own, HALF), -1e30, jnp.float32)], axis=0)
    per = TILE // HALF
    for t in range(KEYS // TILE):
        block = near_ref[t * per : (t + 1) * per, 0].reshape(TILE, HD)
        block = jnp.concatenate([block, key_mask_ref[t * TILE : (t + 1) * TILE, :]], axis=1)
        raw = lax.dot_general(queries, block, across_depth, preferred_element_type=jnp.float32)
        for j in range(per):
            part = raw[:, j * HALF : (j + 1) * HALF]
            first = t * TILE + j * HALF
            raw_ref[:, first : first + HALF] = part
            peak = jnp.maximum(peak, part)
    raw_ref[0:own, pl.ds(pl.multiple_of(slot * HALF, HALF), HALF)] = diagonal
    row_max = jnp.max(peak, axis=1, keepdims=True)
    total = jnp.zeros((ROWS, HALF), jnp.float32)
    for j in range(0, KEYS, HALF):
        probs = jnp.exp2((raw_ref[:, j : j + HALF] - row_max) * SCALE)
        probs_ref[:, j : j + HALF] = probs.astype(jnp.bfloat16)
        total = total + probs
    row_sum = jnp.sum(total, axis=1, keepdims=True)
    first_lane = lax.broadcasted_iota(jnp.int32, (ROWS, HALF), 1) == 0
    stats_ref[...] = jnp.where(first_lane, row_max, row_sum).T[0:2, :]


def row_kernel(probs_ref, near_ref, keep_ref, send_ref):
    acc = jnp.dot(probs_ref[...], near_ref[:, 1].reshape(KEYS, HD), preferred_element_type=jnp.float32)
    for k in range(2):
        keep_ref[k] = acc[2 * k * TOK : (2 * k + 1) * TOK]
        send_ref[k] = acc[(2 * k + 1) * TOK : (2 * k + 2) * TOK]


def stat(ref, k):
    cut = slice(k * TOK, (k + 1) * TOK)
    return ref[0:1, cut], ref[1:2, cut]


def as_column(row):
    return jnp.broadcast_to(row, (HD, TOK)).T


def pair_kernel(mine_ref, core_ref, send_ref, pair_ref):
    for k in range(FLIPS):
        (m0, l0), (m1, l1) = stat(mine_ref, k), stat(core_ref, k ^ 1)
        top = jnp.maximum(m0, m1)
        cut = slice(k * TOK, (k + 1) * TOK)
        pair_ref[0:1, cut] = top
        pair_ref[1:2, cut] = l0 * jnp.exp2((m0 - top) * SCALE) + l1 * jnp.exp2((m1 - top) * SCALE)


def join_kernel(keep_ref, got_ref, mine_ref, core_ref, keep_out_ref, send_ref):
    for k, ref in ((0, keep_out_ref), (2, send_ref)):
        m0, m1 = stat(mine_ref, k)[0], stat(core_ref, k ^ 1)[0]
        top = jnp.maximum(m0, m1)
        w0, w1 = jnp.exp2((m0 - top) * SCALE), jnp.exp2((m1 - top) * SCALE)
        joined = keep_ref[k // 2] * as_column(w0) + got_ref[k // 2] * as_column(w1)
        ref[...] = joined.astype(ref.dtype)


def column_kernel(probs_ref, mine_ref, pair_ref, plane_ref, send_ref, cols_ref):
    weight = []
    for k in range(FLIPS):
        (m0, l0), (m1, l1) = stat(pair_ref, k), stat(plane_ref, k ^ 2)
        top = jnp.maximum(m0, m1)
        norm = l0 * jnp.exp2((m0 - top) * SCALE) + l1 * jnp.exp2((m1 - top) * SCALE)
        weight.append(jnp.exp2((stat(mine_ref, k)[0] - top) * SCALE) / norm)
    weight = jnp.concatenate(weight, axis=1)
    high = weight.astype(jnp.bfloat16).astype(jnp.float32)
    row = lax.broadcasted_iota(jnp.int32, (8, ROWS), 0)
    both = jnp.where(row == 0, high, jnp.where(row == 1, weight - high, 0.0)).astype(jnp.bfloat16)
    for b in range(0, BLOCKS, 2):
        first = b * HALF
        sums = jnp.dot(both, probs_ref[:, first : first + 2 * HALF], preferred_element_type=jnp.float32)
        line = jnp.sum(sums, axis=0, keepdims=True)
        pair = [jnp.broadcast_to(line[:, i * HALF : (i + 1) * HALF], (NZL, HALF)) for i in range(2)]
        cols_ref[b * NZL : (b + 2) * NZL, :] = jnp.concatenate(pair, axis=0)


def merge_kernel(keep_ref, got_ref, pair_ref, plane_ref, out_ref):
    (m0, l0), (m1, l1) = stat(pair_ref, 0), stat(plane_ref, 2)
    top = jnp.maximum(m0, m1)
    w0, w1 = jnp.exp2((m0 - top) * SCALE), jnp.exp2((m1 - top) * SCALE)
    norm = w0 * l0 + w1 * l1
    out = keep_ref[...] * as_column(w0 / norm) + got_ref[...].astype(jnp.float32) * as_column(w1 / norm)
    out_ref[...] = out.astype(jnp.bfloat16)


def kernel(fn, name, shapes, specs, scratch=(), limit=8, space=VMEM, flops=0):
    return pl.pallas_call(
        fn,
        out_shape=shapes,
        in_specs=specs,
        out_specs=jax.tree.map(lambda _: space, shapes),
        scratch_shapes=scratch,
        compiler_params=pltpu.CompilerParams(vmem_limit_bytes=limit * MIB),
        cost_estimate=pl.CostEstimate(flops=flops, bytes_accessed=0, transcendentals=0) if flops else None,
        name=name,
    )


def body(queries, keys, values, doc_lengths):
    shape = jax.ShapeDtypeStruct
    f32, bf16 = jnp.float32, jnp.bfloat16
    def across(x):
        return lax.ppermute(x, "c", [(0, 1), (1, 0)])

    def partner(x):
        return lax.ppermute(x, ("zh", "zl", "c"), [(i, i ^ 12) for i in range(16)])

    copies = kernel(
        spread_kernel,
        "spread",
        shape((BLOCKS, 2, NZL, CHUNK, HD), bf16),
        [ANY] * 2,
        [
            pltpu.VMEM((2, NZL, CHUNK, HD), bf16),
            pltpu.SemaphoreType.DMA((2,)),
            pltpu.SemaphoreType.DMA((BLOCKS,)),
        ],
        limit=60,
        space=ANY,
    )(keys.reshape(NZL, 2, CHUNK, HD), values.reshape(NZL, 2, CHUNK, HD)).reshape(BLOCKS, 2, HALF, HD)
    near = lax.all_to_all(copies, ("y", "x"), 0, 0, tiled=True)
    q1, q2 = across(queries), partner(queries)
    q3 = across(q2)
    own, row_mask, key_mask = kernel(
        limit_kernel,
        "limits",
        (shape((TOK, HD), bf16), shape((ROWS, HD), bf16), shape((KEYS, HD), bf16)),
        [SMEM, VMEM],
    )(doc_lengths, queries)
    near, q1, q2, q3, own, row_mask, key_mask = lax.optimization_barrier(
        (near, q1, q2, q3, own, row_mask, key_mask)
    )
    probs, mine = kernel(
        score_kernel,
        "scores",
        (shape((ROWS, KEYS), bf16), shape((2, ROWS), f32)),
        [VMEM] * 7,
        [pltpu.VMEM((ROWS, KEYS), f32)],
        limit=24,
    )(near, own, q1, q2, q3, row_mask, key_mask)
    core = across(mine)
    keep, send = kernel(row_kernel, "rows", (shape((2, TOK, HD), f32),) * 2, [VMEM] * 2, flops=LONG)(probs, near)
    pair = kernel(pair_kernel, "pair", shape((2, ROWS), f32), [VMEM] * 2 + [ANY], flops=LONG)(mine, core, send)
    plane = partner(pair)
    keep, send = kernel(
        join_kernel, "join", (shape((TOK, HD), f32), shape((TOK, HD), bf16)), [VMEM] * 4, flops=LONG
    )(keep, across(send), mine, core)
    got = partner(send)
    cols = kernel(
        column_kernel, "columns", shape((BLOCKS * NZL, HALF), f32), [VMEM] * 4 + [ANY], flops=LONG
    )(probs, mine, pair, plane, send)
    parts = lax.all_to_all(cols.reshape(BLOCKS * NZL, 1, HALF), ("y", "x", "zl"), 0, 0, tiled=True)
    rows = kernel(merge_kernel, "merge", shape((TOK, HD), bf16), [VMEM] * 4, flops=LONG)(keep, got, pair, plane)
    parts, _ = lax.optimization_barrier((parts, rows))
    totals = (jnp.sum(parts, axis=(0, 1)) / HEADS).reshape(NZL, CHUNK)
    return rows, lax.dynamic_index_in_dim(totals, lax.axis_index("zl"), 0, keepdims=False)


def solution(mesh):
    fine = Mesh(mesh.devices.reshape(tuple(AXES.values())), tuple(AXES))
    ctx, head = ("y", "zh", "x"), ("zl", "c")
    return jax.shard_map(
        body,
        mesh=fine,
        in_specs=(P(ctx, head), P(ctx, None), P(ctx, None), P()),
        out_specs=(P(ctx, head), P(ctx + head)),
        check_vma=False,
    )
```

```python
import functools
import math

import jax
import jax.numpy as jnp
from jax import lax
from jax.experimental import pallas as pl
from jax.experimental.pallas import tpu as pltpu
from jax.sharding import Mesh, PartitionSpec as P

HD = 128
HEADS = 8
AXES = {"y": 4, "zh": 2, "x": 4, "zl": 4, "c": 2}
NX = AXES["x"]
NZL = AXES["zl"]
TOK = 256
CHUNK = TOK // HEADS
HALF = TOK // 2
BLOCKS = AXES["y"] * NX
KEYS = BLOCKS * HALF
FLIPS = 4
ROWS = FLIPS * TOK
TILE = 512
SCALE = math.log2(math.e) / math.sqrt(HD)
OWN, OTHER = 4, 5
BARRED = 32768.0
LONG = 20_000_000_000
MIB = 1024 * 1024
VMEM = pl.BlockSpec(memory_space=pltpu.VMEM)
ANY = pl.BlockSpec(memory_space=pl.ANY)
SMEM = pl.BlockSpec(memory_space=pltpu.SMEM)


def spread_kernel(keys_ref, values_ref, out_ref, piece_ref, in_sems, out_sems):
    c = lax.axis_index("c")
    reads = [
        pltpu.make_async_copy(ref.at[:, c], piece_ref.at[n], in_sems.at[n])
        for n, ref in enumerate((keys_ref, values_ref))
    ]
    for copy in reads:
        copy.start()
    for copy in reads:
        copy.wait()
    writes = [pltpu.make_async_copy(piece_ref, out_ref.at[i], out_sems.at[i]) for i in range(BLOCKS)]
    for copy in writes:
        copy.start()
    for copy in writes:
        copy.wait()


def inside_block(index):
    return (index // CHUNK * 2 + lax.axis_index("c")) * CHUNK + index % CHUNK


def limit_kernel(docs_ref, own_ref, q_ref, row_mask_ref, key_mask_ref):
    q_ref[...] = own_ref[...]
    y, zh, x = (lax.axis_index(a) for a in ("y", "zh", "x"))
    own, other = y * 8 + zh * 4 + x, y * 8 + (1 - zh) * 4 + x
    ends = [docs_ref[0]]
    for i in (1, 2):
        ends.append(ends[-1] + docs_ref[i])

    def document(pos):
        return sum((pos >= end).astype(jnp.int32) for end in ends)

    row = lax.broadcasted_iota(jnp.int32, (ROWS, HD), 0)
    lane = lax.broadcasted_iota(jnp.int32, (ROWS, HD), 1)
    mine = row < 2 * TOK
    doc = document(jnp.where(mine, own, other) * TOK + row % TOK)
    hit = (lane == doc) | (lane == jnp.where(mine, OWN, OTHER))
    row_mask_ref[...] = jnp.where(hit, 1.0, 0.0).astype(jnp.bfloat16)

    key = lax.broadcasted_iota(jnp.int32, (KEYS, HD), 0)
    lane = lax.broadcasted_iota(jnp.int32, (KEYS, HD), 1)
    slot = key // HALF
    block = slot // NX * 8 + zh * 4 + slot % NX
    doc = document(block * TOK + inside_block(key % HALF))
    barred = (lane < OWN) & (lane != doc)
    barred = barred | ((lane == OWN) & (block >= own)) | ((lane == OTHER) & (block > other))
    key_mask_ref[...] = jnp.where(barred, -BARRED, 0.0).astype(jnp.bfloat16)


def score_kernel(near_ref, q0, q1, q2, q3, row_mask_ref, key_mask_ref, probs_ref, stats_ref, raw_ref):
    across_depth = (((1,), (1,)), ((), ()))
    queries = jnp.concatenate([q[...] for q in (q0, q1, q2, q3)], axis=0)
    queries = jnp.concatenate([queries, row_mask_ref[...]], axis=1)
    own = 2 * TOK
    slot = lax.axis_index("y") * NX + lax.axis_index("x")
    mask = key_mask_ref[pl.ds(pl.multiple_of(slot * HALF, HALF), HALF), :]
    feature = lax.broadcasted_iota(jnp.int32, (HALF, HD), 1)
    mask = jnp.where(feature == OWN, 0.0, mask.astype(jnp.float32)).astype(jnp.bfloat16)
    block = jnp.concatenate([near_ref[slot, 0], mask], axis=1)
    diagonal = lax.dot_general(queries[:own], block, across_depth, preferred_element_type=jnp.float32)
    row = lax.broadcasted_iota(jnp.int32, (own, HALF), 0) % TOK
    lane = lax.broadcasted_iota(jnp.int32, (own, HALF), 1)
    diagonal = jnp.where(inside_block(lane) <= row, diagonal, -jnp.inf)
    peak = jnp.maximum(jnp.full((own, HALF), -1e30, jnp.float32), diagonal)
    peak = jnp.concatenate([peak, jnp.full((ROWS - own, HALF), -1e30, jnp.float32)], axis=0)
    per = TILE // HALF
    for t in range(KEYS // TILE):
        block = near_ref[t * per : (t + 1) * per, 0].reshape(TILE, HD)
        block = jnp.concatenate([block, key_mask_ref[t * TILE : (t + 1) * TILE, :]], axis=1)
        raw = lax.dot_general(queries, block, across_depth, preferred_element_type=jnp.float32)
        for j in range(per):
            part = raw[:, j * HALF : (j + 1) * HALF]
            first = t * TILE + j * HALF
            raw_ref[:, first : first + HALF] = part
            peak = jnp.maximum(peak, part)
    raw_ref[0:own, pl.ds(pl.multiple_of(slot * HALF, HALF), HALF)] = diagonal
    row_max = jnp.max(peak, axis=1, keepdims=True)
    total = jnp.zeros((ROWS, HALF), jnp.float32)
    for j in range(0, KEYS, HALF):
        probs = jnp.exp2((raw_ref[:, j : j + HALF] - row_max) * SCALE)
        probs_ref[:, j : j + HALF] = probs.astype(jnp.bfloat16)
        total = total + probs
    row_sum = jnp.sum(total, axis=1, keepdims=True)
    first_lane = lax.broadcasted_iota(jnp.int32, (ROWS, HALF), 1) == 0
    stats_ref[...] = jnp.where(first_lane, row_max, row_sum).T[0:2, :]


def row_kernel(first, probs_ref, near_ref, after_ref, out_ref):
    values = near_ref[:, 1].reshape(KEYS, HD)
    for k in range(2):
        rows = slice((2 * k + first) * TOK, (2 * k + first + 1) * TOK)
        out_ref[k] = jnp.dot(probs_ref[rows, :], values, preferred_element_type=jnp.float32)


def stat(ref, k):
    cut = slice(k * TOK, (k + 1) * TOK)
    return ref[0:1, cut], ref[1:2, cut]


def as_column(row):
    return jnp.broadcast_to(row, (HD, TOK)).T


def pair_kernel(mine_ref, core_ref, send_ref, pair_ref):
    for k in range(FLIPS):
        (m0, l0), (m1, l1) = stat(mine_ref, k), stat(core_ref, k ^ 1)
        top = jnp.maximum(m0, m1)
        cut = slice(k * TOK, (k + 1) * TOK)
        pair_ref[0:1, cut] = top
        pair_ref[1:2, cut] = l0 * jnp.exp2((m0 - top) * SCALE) + l1 * jnp.exp2((m1 - top) * SCALE)


def join_kernel(keep_ref, got_ref, mine_ref, core_ref, keep_out_ref, send_ref):
    for k, ref in ((0, keep_out_ref), (2, send_ref)):
        m0, m1 = stat(mine_ref, k)[0], stat(core_ref, k ^ 1)[0]
        top = jnp.maximum(m0, m1)
        w0, w1 = jnp.exp2((m0 - top) * SCALE), jnp.exp2((m1 - top) * SCALE)
        joined = keep_ref[k // 2] * as_column(w0) + got_ref[k // 2] * as_column(w1)
        ref[...] = joined.astype(ref.dtype)


def column_kernel(probs_ref, mine_ref, pair_ref, plane_ref, send_ref, cols_ref):
    weight = []
    for k in range(FLIPS):
        (m0, l0), (m1, l1) = stat(pair_ref, k), stat(plane_ref, k ^ 2)
        top = jnp.maximum(m0, m1)
        norm = l0 * jnp.exp2((m0 - top) * SCALE) + l1 * jnp.exp2((m1 - top) * SCALE)
        weight.append(jnp.exp2((stat(mine_ref, k)[0] - top) * SCALE) / norm)
    weight = jnp.concatenate(weight, axis=1)
    high = weight.astype(jnp.bfloat16).astype(jnp.float32)
    row = lax.broadcasted_iota(jnp.int32, (8, ROWS), 0)
    both = jnp.where(row == 0, high, jnp.where(row == 1, weight - high, 0.0)).astype(jnp.bfloat16)
    for b in range(0, BLOCKS, 2):
        first = b * HALF
        sums = jnp.dot(both, probs_ref[:, first : first + 2 * HALF], preferred_element_type=jnp.float32)
        line = jnp.sum(sums, axis=0, keepdims=True)
        pair = [jnp.broadcast_to(line[:, i * HALF : (i + 1) * HALF], (NZL, HALF)) for i in range(2)]
        cols_ref[b * NZL : (b + 2) * NZL, :] = jnp.concatenate(pair, axis=0)


def merge_kernel(keep_ref, got_ref, pair_ref, plane_ref, out_ref):
    (m0, l0), (m1, l1) = stat(pair_ref, 0), stat(plane_ref, 2)
    top = jnp.maximum(m0, m1)
    w0, w1 = jnp.exp2((m0 - top) * SCALE), jnp.exp2((m1 - top) * SCALE)
    norm = w0 * l0 + w1 * l1
    out = keep_ref[...] * as_column(w0 / norm) + got_ref[...].astype(jnp.float32) * as_column(w1 / norm)
    out_ref[...] = out.astype(jnp.bfloat16)


def kernel(fn, name, shapes, specs, scratch=(), limit=8, space=VMEM, flops=0):
    return pl.pallas_call(
        fn,
        out_shape=shapes,
        in_specs=specs,
        out_specs=jax.tree.map(lambda _: space, shapes),
        scratch_shapes=scratch,
        compiler_params=pltpu.CompilerParams(vmem_limit_bytes=limit * MIB),
        cost_estimate=pl.CostEstimate(flops=flops, bytes_accessed=0, transcendentals=0) if flops else None,
        name=name,
    )


def body(queries, keys, values, doc_lengths):
    shape = jax.ShapeDtypeStruct
    f32, bf16 = jnp.float32, jnp.bfloat16
    def across(x):
        return lax.ppermute(x, "c", [(0, 1), (1, 0)])

    def partner(x):
        return lax.ppermute(x, ("zh", "zl", "c"), [(i, i ^ 12) for i in range(16)])

    copies = kernel(
        spread_kernel,
        "spread",
        shape((BLOCKS, 2, NZL, CHUNK, HD), bf16),
        [ANY] * 2,
        [
            pltpu.VMEM((2, NZL, CHUNK, HD), bf16),
            pltpu.SemaphoreType.DMA((2,)),
            pltpu.SemaphoreType.DMA((BLOCKS,)),
        ],
        limit=60,
        space=ANY,
    )(keys.reshape(NZL, 2, CHUNK, HD), values.reshape(NZL, 2, CHUNK, HD)).reshape(BLOCKS, 2, HALF, HD)
    near = lax.all_to_all(copies, ("y", "x"), 0, 0, tiled=True)
    q1, q2 = across(queries), partner(queries)
    q3 = across(q2)
    own, row_mask, key_mask = kernel(
        limit_kernel,
        "limits",
        (shape((TOK, HD), bf16), shape((ROWS, HD), bf16), shape((KEYS, HD), bf16)),
        [SMEM, VMEM],
    )(doc_lengths, queries)
    near, q1, q2, q3, own, row_mask, key_mask = lax.optimization_barrier(
        (near, q1, q2, q3, own, row_mask, key_mask)
    )
    probs, mine = kernel(
        score_kernel,
        "scores",
        (shape((ROWS, KEYS), bf16), shape((2, ROWS), f32)),
        [VMEM] * 7,
        [pltpu.VMEM((ROWS, KEYS), f32)],
        limit=24,
    )(near, own, q1, q2, q3, row_mask, key_mask)
    core = across(mine)
    half = shape((2, TOK, HD), f32)
    send = kernel(functools.partial(row_kernel, 1), "rows_out", half, [VMEM] * 2 + [ANY], flops=LONG)(
        probs, near, mine
    )
    pair = kernel(pair_kernel, "pair", shape((2, ROWS), f32), [VMEM] * 2 + [ANY], flops=LONG)(mine, core, send)
    plane = partner(pair)
    joined = across(send)
    keep = kernel(functools.partial(row_kernel, 0), "rows_kept", half, [VMEM] * 2 + [ANY], flops=LONG)(
        probs, near, joined
    )
    keep, send = kernel(
        join_kernel, "join", (shape((TOK, HD), f32), shape((TOK, HD), bf16)), [VMEM] * 4, flops=LONG
    )(keep, joined, mine, core)
    got = partner(send)
    cols = kernel(
        column_kernel, "columns", shape((BLOCKS * NZL, HALF), f32), [VMEM] * 4 + [ANY], flops=LONG
    )(probs, mine, pair, plane, send)
    parts = lax.all_to_all(cols.reshape(BLOCKS * NZL, 1, HALF), ("y", "x", "zl"), 0, 0, tiled=True)
    rows = kernel(merge_kernel, "merge", shape((TOK, HD), bf16), [VMEM] * 4, flops=LONG)(keep, got, pair, plane)
    parts, _ = lax.optimization_barrier((parts, rows))
    piece = lax.dynamic_slice_in_dim(parts.reshape(BLOCKS * NZL, HALF), lax.axis_index("zl") * CHUNK, CHUNK, axis=1)
    return rows, jnp.sum(piece, axis=0) / HEADS


def solution(mesh):
    fine = Mesh(mesh.devices.reshape(tuple(AXES.values())), tuple(AXES))
    ctx, head = ("y", "zh", "x"), ("zl", "c")
    return jax.shard_map(
        body,
        mesh=fine,
        in_specs=(P(ctx, head), P(ctx, None), P(ctx, None), P()),
        out_specs=(P(ctx, head), P(ctx + head)),
        check_vma=False,
    )
```

```python
import math

import jax
import jax.numpy as jnp
from jax import lax
from jax.experimental import pallas as pl
from jax.experimental.pallas import tpu as pltpu
from jax.sharding import Mesh, PartitionSpec as P

HD = 128
HEADS = 8
AXES = {"y": 4, "zh": 2, "x": 4, "zl": 4, "c": 2}
NX = AXES["x"]
NZL = AXES["zl"]
TOK = 256
CHUNK = TOK // HEADS
HALF = TOK // 2
BLOCKS = AXES["y"] * NX
KEYS = BLOCKS * HALF
FLIPS = 4
ROWS = FLIPS * TOK
TILE = 512
SCALE = math.log2(math.e) / math.sqrt(HD)
OWN, OTHER = 4, 5
BARRED = 32768.0
LONG = 20_000_000_000
MIB = 1024 * 1024
VMEM = pl.BlockSpec(memory_space=pltpu.VMEM)
ANY = pl.BlockSpec(memory_space=pl.ANY)
SMEM = pl.BlockSpec(memory_space=pltpu.SMEM)


def spread_kernel(keys_ref, values_ref, out_ref, piece_ref, in_sems, out_sems):
    c = lax.axis_index("c")
    reads = [
        pltpu.make_async_copy(ref.at[:, c], piece_ref.at[n], in_sems.at[n])
        for n, ref in enumerate((keys_ref, values_ref))
    ]
    for copy in reads:
        copy.start()
    for copy in reads:
        copy.wait()
    writes = [pltpu.make_async_copy(piece_ref, out_ref.at[i], out_sems.at[i]) for i in range(BLOCKS)]
    for copy in writes:
        copy.start()
    for copy in writes:
        copy.wait()


def inside_block(index):
    return (index // CHUNK * 2 + lax.axis_index("c")) * CHUNK + index % CHUNK


def limit_kernel(docs_ref, own_ref, q_ref, row_mask_ref, key_mask_ref):
    q_ref[...] = own_ref[...]
    y, zh, x = (lax.axis_index(a) for a in ("y", "zh", "x"))
    own, other = y * 8 + zh * 4 + x, y * 8 + (1 - zh) * 4 + x
    ends = [docs_ref[0]]
    for i in (1, 2):
        ends.append(ends[-1] + docs_ref[i])

    def document(pos):
        return sum((pos >= end).astype(jnp.int32) for end in ends)

    row = lax.broadcasted_iota(jnp.int32, (ROWS, HD), 0)
    lane = lax.broadcasted_iota(jnp.int32, (ROWS, HD), 1)
    mine = row < 2 * TOK
    doc = document(jnp.where(mine, own, other) * TOK + row % TOK)
    hit = (lane == doc) | (lane == jnp.where(mine, OWN, OTHER))
    row_mask_ref[...] = jnp.where(hit, 1.0, 0.0).astype(jnp.bfloat16)

    key = lax.broadcasted_iota(jnp.int32, (KEYS, HD), 0)
    lane = lax.broadcasted_iota(jnp.int32, (KEYS, HD), 1)
    slot = key // HALF
    block = slot // NX * 8 + zh * 4 + slot % NX
    doc = document(block * TOK + inside_block(key % HALF))
    barred = (lane < OWN) & (lane != doc)
    barred = barred | ((lane == OWN) & (block >= own)) | ((lane == OTHER) & (block > other))
    key_mask_ref[...] = jnp.where(barred, -BARRED, 0.0).astype(jnp.bfloat16)


def score_kernel(near_ref, q0, q1, q2, q3, row_mask_ref, key_mask_ref, probs_ref, stats_ref, raw_ref):
    across_depth = (((1,), (1,)), ((), ()))
    queries = jnp.concatenate([q[...] for q in (q0, q1, q2, q3)], axis=0)
    queries = jnp.concatenate([queries, row_mask_ref[...]], axis=1)
    own = 2 * TOK
    slot = lax.axis_index("y") * NX + lax.axis_index("x")
    mask = key_mask_ref[pl.ds(pl.multiple_of(slot * HALF, HALF), HALF), :]
    feature = lax.broadcasted_iota(jnp.int32, (HALF, HD), 1)
    mask = jnp.where(feature == OWN, 0.0, mask.astype(jnp.float32)).astype(jnp.bfloat16)
    block = jnp.concatenate([near_ref[slot, 0], mask], axis=1)
    diagonal = lax.dot_general(queries[:own], block, across_depth, preferred_element_type=jnp.float32)
    row = lax.broadcasted_iota(jnp.int32, (own, HALF), 0) % TOK
    lane = lax.broadcasted_iota(jnp.int32, (own, HALF), 1)
    diagonal = jnp.where(inside_block(lane) <= row, diagonal, -jnp.inf)
    peak = jnp.maximum(jnp.full((own, HALF), -1e30, jnp.float32), diagonal)
    peak = jnp.concatenate([peak, jnp.full((ROWS - own, HALF), -1e30, jnp.float32)], axis=0)
    per = TILE // HALF
    for t in range(KEYS // TILE):
        block = near_ref[t * per : (t + 1) * per, 0].reshape(TILE, HD)
        block = jnp.concatenate([block, key_mask_ref[t * TILE : (t + 1) * TILE, :]], axis=1)
        raw = lax.dot_general(queries, block, across_depth, preferred_element_type=jnp.float32)
        for j in range(per):
            part = raw[:, j * HALF : (j + 1) * HALF]
            first = t * TILE + j * HALF
            raw_ref[:, first : first + HALF] = part
            peak = jnp.maximum(peak, part)
    raw_ref[0:own, pl.ds(pl.multiple_of(slot * HALF, HALF), HALF)] = diagonal
    row_max = jnp.max(peak, axis=1, keepdims=True)
    total = jnp.zeros((ROWS, HALF), jnp.float32)
    for j in range(0, KEYS, HALF):
        probs = jnp.exp2((raw_ref[:, j : j + HALF] - row_max) * SCALE)
        probs_ref[:, j : j + HALF] = probs.astype(jnp.bfloat16)
        total = total + probs
    row_sum = jnp.sum(total, axis=1, keepdims=True)
    first_lane = lax.broadcasted_iota(jnp.int32, (ROWS, HALF), 1) == 0
    stats_ref[...] = jnp.where(first_lane, row_max, row_sum).T[0:2, :]


def weighted(probs_ref, near_ref, k):
    values = near_ref[:, 1].reshape(KEYS, HD)
    return jnp.dot(probs_ref[k * TOK : (k + 1) * TOK, :], values, preferred_element_type=jnp.float32)


def send_kernel(probs_ref, near_ref, send_ref):
    for k in range(2):
        send_ref[k] = weighted(probs_ref, near_ref, 2 * k + 1)


def stat(ref, k):
    cut = slice(k * TOK, (k + 1) * TOK)
    return ref[0:1, cut], ref[1:2, cut]


def as_column(row):
    return jnp.broadcast_to(row, (HD, TOK)).T


def pair_kernel(mine_ref, core_ref, send_ref, pair_ref):
    for k in range(FLIPS):
        (m0, l0), (m1, l1) = stat(mine_ref, k), stat(core_ref, k ^ 1)
        top = jnp.maximum(m0, m1)
        cut = slice(k * TOK, (k + 1) * TOK)
        pair_ref[0:1, cut] = top
        pair_ref[1:2, cut] = l0 * jnp.exp2((m0 - top) * SCALE) + l1 * jnp.exp2((m1 - top) * SCALE)


def join_kernel(probs_ref, near_ref, got_ref, mine_ref, core_ref, keep_ref, send_ref):
    for k, ref in ((0, keep_ref), (2, send_ref)):
        m0, m1 = stat(mine_ref, k)[0], stat(core_ref, k ^ 1)[0]
        top = jnp.maximum(m0, m1)
        w0, w1 = jnp.exp2((m0 - top) * SCALE), jnp.exp2((m1 - top) * SCALE)
        joined = weighted(probs_ref, near_ref, k) * as_column(w0) + got_ref[k // 2] * as_column(w1)
        ref[...] = joined.astype(ref.dtype)


def column_kernel(probs_ref, mine_ref, pair_ref, plane_ref, send_ref, cols_ref):
    weight = []
    for k in range(FLIPS):
        (m0, l0), (m1, l1) = stat(pair_ref, k), stat(plane_ref, k ^ 2)
        top = jnp.maximum(m0, m1)
        norm = l0 * jnp.exp2((m0 - top) * SCALE) + l1 * jnp.exp2((m1 - top) * SCALE)
        weight.append(jnp.exp2((stat(mine_ref, k)[0] - top) * SCALE) / norm)
    weight = jnp.concatenate(weight, axis=1)
    high = weight.astype(jnp.bfloat16).astype(jnp.float32)
    row = lax.broadcasted_iota(jnp.int32, (8, ROWS), 0)
    both = jnp.where(row == 0, high, jnp.where(row == 1, weight - high, 0.0)).astype(jnp.bfloat16)
    for b in range(0, BLOCKS, 2):
        first = b * HALF
        sums = jnp.dot(both, probs_ref[:, first : first + 2 * HALF], preferred_element_type=jnp.float32)
        line = jnp.sum(sums, axis=0, keepdims=True)
        pair = [jnp.broadcast_to(line[:, i * HALF : (i + 1) * HALF], (NZL, HALF)) for i in range(2)]
        cols_ref[b * NZL : (b + 2) * NZL, :] = jnp.concatenate(pair, axis=0)


def merge_kernel(keep_ref, got_ref, pair_ref, plane_ref, out_ref):
    (m0, l0), (m1, l1) = stat(pair_ref, 0), stat(plane_ref, 2)
    top = jnp.maximum(m0, m1)
    w0, w1 = jnp.exp2((m0 - top) * SCALE), jnp.exp2((m1 - top) * SCALE)
    norm = w0 * l0 + w1 * l1
    out = keep_ref[...] * as_column(w0 / norm) + got_ref[...].astype(jnp.float32) * as_column(w1 / norm)
    out_ref[...] = out.astype(jnp.bfloat16)


def kernel(fn, name, shapes, specs, scratch=(), limit=8, space=VMEM, flops=0):
    return pl.pallas_call(
        fn,
        out_shape=shapes,
        in_specs=specs,
        out_specs=jax.tree.map(lambda _: space, shapes),
        scratch_shapes=scratch,
        compiler_params=pltpu.CompilerParams(vmem_limit_bytes=limit * MIB),
        cost_estimate=pl.CostEstimate(flops=flops, bytes_accessed=0, transcendentals=0) if flops else None,
        name=name,
    )


def body(queries, keys, values, doc_lengths):
    shape = jax.ShapeDtypeStruct
    f32, bf16 = jnp.float32, jnp.bfloat16
    def across(x):
        return lax.ppermute(x, "c", [(0, 1), (1, 0)])

    def partner(x):
        return lax.ppermute(x, ("zh", "zl", "c"), [(i, i ^ 12) for i in range(16)])

    copies = kernel(
        spread_kernel,
        "spread",
        shape((BLOCKS, 2, NZL, CHUNK, HD), bf16),
        [ANY] * 2,
        [
            pltpu.VMEM((2, NZL, CHUNK, HD), bf16),
            pltpu.SemaphoreType.DMA((2,)),
            pltpu.SemaphoreType.DMA((BLOCKS,)),
        ],
        limit=60,
        space=ANY,
    )(keys.reshape(NZL, 2, CHUNK, HD), values.reshape(NZL, 2, CHUNK, HD)).reshape(BLOCKS, 2, HALF, HD)
    near = lax.all_to_all(copies, ("y", "x"), 0, 0, tiled=True)
    q1, q2 = across(queries), partner(queries)
    q3 = across(q2)
    own, row_mask, key_mask = kernel(
        limit_kernel,
        "limits",
        (shape((TOK, HD), bf16), shape((ROWS, HD), bf16), shape((KEYS, HD), bf16)),
        [SMEM, VMEM],
    )(doc_lengths, queries)
    near, q1, q2, q3, own, row_mask, key_mask = lax.optimization_barrier(
        (near, q1, q2, q3, own, row_mask, key_mask)
    )
    probs, mine = kernel(
        score_kernel,
        "scores",
        (shape((ROWS, KEYS), bf16), shape((2, ROWS), f32)),
        [VMEM] * 7,
        [pltpu.VMEM((ROWS, KEYS), f32)],
        limit=24,
    )(near, own, q1, q2, q3, row_mask, key_mask)
    core = across(mine)
    send = kernel(send_kernel, "rows_sent", shape((2, TOK, HD), f32), [VMEM] * 2, flops=LONG)(probs, near)
    pair = kernel(pair_kernel, "pair", shape((2, ROWS), f32), [VMEM] * 2 + [ANY], flops=LONG)(mine, core, send)
    plane = partner(pair)
    keep, send = kernel(
        join_kernel, "rows_joined", (shape((TOK, HD), f32), shape((TOK, HD), bf16)), [VMEM] * 5, flops=LONG
    )(probs, near, across(send), mine, core)
    got = partner(send)
    cols = kernel(
        column_kernel, "columns", shape((BLOCKS * NZL, HALF), f32), [VMEM] * 4 + [ANY], flops=LONG
    )(probs, mine, pair, plane, send)
    parts = lax.all_to_all(cols.reshape(BLOCKS * NZL, 1, HALF), ("y", "x", "zl"), 0, 0, tiled=True)
    rows = kernel(merge_kernel, "merge", shape((TOK, HD), bf16), [VMEM] * 4, flops=LONG)(keep, got, pair, plane)
    parts, _ = lax.optimization_barrier((parts, rows))
    piece = lax.dynamic_slice_in_dim(parts.reshape(BLOCKS * NZL, HALF), lax.axis_index("zl") * CHUNK, CHUNK, axis=1)
    return rows, jnp.sum(piece, axis=0) / HEADS


def solution(mesh):
    fine = Mesh(mesh.devices.reshape(tuple(AXES.values())), tuple(AXES))
    ctx, head = ("y", "zh", "x"), ("zl", "c")
    return jax.shard_map(
        body,
        mesh=fine,
        in_specs=(P(ctx, head), P(ctx, None), P(ctx, None), P()),
        out_specs=(P(ctx, head), P(ctx + head)),
        check_vma=False,
    )
```

```python
import math

import jax
import jax.numpy as jnp
from jax import lax
from jax.experimental import pallas as pl
from jax.experimental.pallas import tpu as pltpu
from jax.sharding import Mesh, PartitionSpec as P

HD = 128
HEADS = 8
AXES = {"y": 4, "zh": 2, "x": 4, "zl": 4, "c": 2}
NX = AXES["x"]
NZL = AXES["zl"]
TOK = 256
CHUNK = TOK // HEADS
HALF = TOK // 2
BLOCKS = AXES["y"] * NX
KEYS = BLOCKS * HALF
FLIPS = 4
ROWS = FLIPS * TOK
TILE = 512
SCALE = math.log2(math.e) / math.sqrt(HD)
OWN, OTHER = 4, 5
BARRED = 32768.0
LONG = 20_000_000_000
MIB = 1024 * 1024
VMEM = pl.BlockSpec(memory_space=pltpu.VMEM)
ANY = pl.BlockSpec(memory_space=pl.ANY)
SMEM = pl.BlockSpec(memory_space=pltpu.SMEM)


def spread_kernel(keys_ref, values_ref, out_ref, piece_ref, in_sems, out_sems):
    c = lax.axis_index("c")
    reads = [
        pltpu.make_async_copy(ref.at[:, c], piece_ref.at[n], in_sems.at[n])
        for n, ref in enumerate((keys_ref, values_ref))
    ]
    for copy in reads:
        copy.start()
    for copy in reads:
        copy.wait()
    writes = [pltpu.make_async_copy(piece_ref, out_ref.at[i], out_sems.at[i]) for i in range(BLOCKS)]
    for copy in writes:
        copy.start()
    for copy in writes:
        copy.wait()


def inside_block(index):
    return (index // CHUNK * 2 + lax.axis_index("c")) * CHUNK + index % CHUNK


def limit_kernel(docs_ref, own_ref, q_ref, row_mask_ref, key_mask_ref):
    q_ref[...] = own_ref[...]
    y, zh, x = (lax.axis_index(a) for a in ("y", "zh", "x"))
    own, other = y * 8 + zh * 4 + x, y * 8 + (1 - zh) * 4 + x
    ends = [docs_ref[0]]
    for i in (1, 2):
        ends.append(ends[-1] + docs_ref[i])

    def document(pos):
        return sum((pos >= end).astype(jnp.int32) for end in ends)

    row = lax.broadcasted_iota(jnp.int32, (ROWS, HD), 0)
    lane = lax.broadcasted_iota(jnp.int32, (ROWS, HD), 1)
    mine = row < 2 * TOK
    doc = document(jnp.where(mine, own, other) * TOK + row % TOK)
    hit = (lane == doc) | (lane == jnp.where(mine, OWN, OTHER))
    row_mask_ref[...] = jnp.where(hit, 1.0, 0.0).astype(jnp.bfloat16)

    key = lax.broadcasted_iota(jnp.int32, (KEYS, HD), 0)
    lane = lax.broadcasted_iota(jnp.int32, (KEYS, HD), 1)
    slot = key // HALF
    block = slot // NX * 8 + zh * 4 + slot % NX
    doc = document(block * TOK + inside_block(key % HALF))
    barred = (lane < OWN) & (lane != doc)
    barred = barred | ((lane == OWN) & (block >= own)) | ((lane == OTHER) & (block > other))
    key_mask_ref[...] = jnp.where(barred, -BARRED, 0.0).astype(jnp.bfloat16)


def score_kernel(near_ref, q0, q1, q2, q3, row_mask_ref, key_mask_ref, probs_ref, stats_ref, raw_ref):
    across_depth = (((1,), (1,)), ((), ()))
    queries = jnp.concatenate([q[...] for q in (q0, q1, q2, q3)], axis=0)
    queries = jnp.concatenate([queries, row_mask_ref[...]], axis=1)
    own = 2 * TOK
    slot = lax.axis_index("y") * NX + lax.axis_index("x")
    mask = key_mask_ref[pl.ds(pl.multiple_of(slot * HALF, HALF), HALF), :]
    feature = lax.broadcasted_iota(jnp.int32, (HALF, HD), 1)
    mask = jnp.where(feature == OWN, 0.0, mask.astype(jnp.float32)).astype(jnp.bfloat16)
    block = jnp.concatenate([near_ref[slot, 0], mask], axis=1)
    diagonal = lax.dot_general(queries[:own], block, across_depth, preferred_element_type=jnp.float32)
    row = lax.broadcasted_iota(jnp.int32, (own, HALF), 0) % TOK
    lane = lax.broadcasted_iota(jnp.int32, (own, HALF), 1)
    diagonal = jnp.where(inside_block(lane) <= row, diagonal, -jnp.inf)
    peak = jnp.maximum(jnp.full((own, HALF), -1e30, jnp.float32), diagonal)
    peak = jnp.concatenate([peak, jnp.full((ROWS - own, HALF), -1e30, jnp.float32)], axis=0)
    per = TILE // HALF
    for t in range(KEYS // TILE):
        block = near_ref[t * per : (t + 1) * per, 0].reshape(TILE, HD)
        block = jnp.concatenate([block, key_mask_ref[t * TILE : (t + 1) * TILE, :]], axis=1)
        raw = lax.dot_general(queries, block, across_depth, preferred_element_type=jnp.float32)
        for j in range(per):
            part = raw[:, j * HALF : (j + 1) * HALF]
            first = t * TILE + j * HALF
            raw_ref[:, first : first + HALF] = part
            peak = jnp.maximum(peak, part)
    raw_ref[0:own, pl.ds(pl.multiple_of(slot * HALF, HALF), HALF)] = diagonal
    row_max = jnp.max(peak, axis=1, keepdims=True)
    total = jnp.zeros((ROWS, HALF), jnp.float32)
    for j in range(0, KEYS, HALF):
        probs = jnp.exp2((raw_ref[:, j : j + HALF] - row_max) * SCALE)
        probs_ref[:, j : j + HALF] = probs.astype(jnp.bfloat16)
        total = total + probs
    row_sum = jnp.sum(total, axis=1, keepdims=True)
    first_lane = lax.broadcasted_iota(jnp.int32, (ROWS, HALF), 1) == 0
    stats_ref[...] = jnp.where(first_lane, row_max, row_sum).T[0:2, :]


def weighted(probs_ref, near_ref, k):
    values = near_ref[:, 1].reshape(KEYS, HD)
    return jnp.dot(probs_ref[k * TOK : (k + 1) * TOK, :], values, preferred_element_type=jnp.float32)


def send_kernel(probs_ref, near_ref, send_ref):
    for k in range(2):
        send_ref[k] = weighted(probs_ref, near_ref, 2 * k + 1).astype(jnp.bfloat16)


def stat(ref, k):
    cut = slice(k * TOK, (k + 1) * TOK)
    return ref[0:1, cut], ref[1:2, cut]


def as_column(row):
    return jnp.broadcast_to(row, (HD, TOK)).T


def pair_kernel(mine_ref, core_ref, send_ref, pair_ref):
    for k in range(FLIPS):
        (m0, l0), (m1, l1) = stat(mine_ref, k), stat(core_ref, k ^ 1)
        top = jnp.maximum(m0, m1)
        cut = slice(k * TOK, (k + 1) * TOK)
        pair_ref[0:1, cut] = top
        pair_ref[1:2, cut] = l0 * jnp.exp2((m0 - top) * SCALE) + l1 * jnp.exp2((m1 - top) * SCALE)


def join_kernel(probs_ref, near_ref, got_ref, mine_ref, core_ref, keep_ref, send_ref):
    for k, ref in ((0, keep_ref), (2, send_ref)):
        m0, m1 = stat(mine_ref, k)[0], stat(core_ref, k ^ 1)[0]
        top = jnp.maximum(m0, m1)
        w0, w1 = jnp.exp2((m0 - top) * SCALE), jnp.exp2((m1 - top) * SCALE)
        joined = weighted(probs_ref, near_ref, k) * as_column(w0) + got_ref[k // 2].astype(jnp.float32) * as_column(w1)
        ref[...] = joined.astype(ref.dtype)


def column_kernel(probs_ref, mine_ref, pair_ref, plane_ref, send_ref, cols_ref):
    weight = []
    for k in range(FLIPS):
        (m0, l0), (m1, l1) = stat(pair_ref, k), stat(plane_ref, k ^ 2)
        top = jnp.maximum(m0, m1)
        norm = l0 * jnp.exp2((m0 - top) * SCALE) + l1 * jnp.exp2((m1 - top) * SCALE)
        weight.append(jnp.exp2((stat(mine_ref, k)[0] - top) * SCALE) / norm)
    weight = jnp.concatenate(weight, axis=1)
    high = weight.astype(jnp.bfloat16).astype(jnp.float32)
    row = lax.broadcasted_iota(jnp.int32, (8, ROWS), 0)
    both = jnp.where(row == 0, high, jnp.where(row == 1, weight - high, 0.0)).astype(jnp.bfloat16)
    for b in range(0, BLOCKS, 2):
        first = b * HALF
        sums = jnp.dot(both, probs_ref[:, first : first + 2 * HALF], preferred_element_type=jnp.float32)
        line = jnp.sum(sums, axis=0, keepdims=True)
        pair = [jnp.broadcast_to(line[:, i * HALF : (i + 1) * HALF], (NZL, HALF)) for i in range(2)]
        cols_ref[b * NZL : (b + 2) * NZL, :] = jnp.concatenate(pair, axis=0)


def merge_kernel(keep_ref, got_ref, pair_ref, plane_ref, out_ref):
    (m0, l0), (m1, l1) = stat(pair_ref, 0), stat(plane_ref, 2)
    top = jnp.maximum(m0, m1)
    w0, w1 = jnp.exp2((m0 - top) * SCALE), jnp.exp2((m1 - top) * SCALE)
    norm = w0 * l0 + w1 * l1
    out = keep_ref[...] * as_column(w0 / norm) + got_ref[...].astype(jnp.float32) * as_column(w1 / norm)
    out_ref[...] = out.astype(jnp.bfloat16)


def kernel(fn, name, shapes, specs, scratch=(), limit=8, space=VMEM, flops=0):
    return pl.pallas_call(
        fn,
        out_shape=shapes,
        in_specs=specs,
        out_specs=jax.tree.map(lambda _: space, shapes),
        scratch_shapes=scratch,
        compiler_params=pltpu.CompilerParams(vmem_limit_bytes=limit * MIB),
        cost_estimate=pl.CostEstimate(flops=flops, bytes_accessed=0, transcendentals=0) if flops else None,
        name=name,
    )


def body(queries, keys, values, doc_lengths):
    shape = jax.ShapeDtypeStruct
    f32, bf16 = jnp.float32, jnp.bfloat16
    def across(x):
        return lax.ppermute(x, "c", [(0, 1), (1, 0)])

    def partner(x):
        return lax.ppermute(x, ("zh", "zl", "c"), [(i, i ^ 12) for i in range(16)])

    copies = kernel(
        spread_kernel,
        "spread",
        shape((BLOCKS, 2, NZL, CHUNK, HD), bf16),
        [ANY] * 2,
        [
            pltpu.VMEM((2, NZL, CHUNK, HD), bf16),
            pltpu.SemaphoreType.DMA((2,)),
            pltpu.SemaphoreType.DMA((BLOCKS,)),
        ],
        limit=60,
        space=ANY,
    )(keys.reshape(NZL, 2, CHUNK, HD), values.reshape(NZL, 2, CHUNK, HD)).reshape(BLOCKS, 2, HALF, HD)
    near = lax.all_to_all(copies, ("y", "x"), 0, 0, tiled=True)
    q1, q2 = across(queries), partner(queries)
    q3 = across(q2)
    own, row_mask, key_mask = kernel(
        limit_kernel,
        "limits",
        (shape((TOK, HD), bf16), shape((ROWS, HD), bf16), shape((KEYS, HD), bf16)),
        [SMEM, VMEM],
    )(doc_lengths, queries)
    near, q1, q2, q3, own, row_mask, key_mask = lax.optimization_barrier(
        (near, q1, q2, q3, own, row_mask, key_mask)
    )
    probs, mine = kernel(
        score_kernel,
        "scores",
        (shape((ROWS, KEYS), bf16), shape((2, ROWS), f32)),
        [VMEM] * 7,
        [pltpu.VMEM((ROWS, KEYS), f32)],
        limit=24,
    )(near, own, q1, q2, q3, row_mask, key_mask)
    core = across(mine)
    send = kernel(send_kernel, "rows_sent", shape((2, TOK, HD), bf16), [VMEM] * 2, flops=LONG)(probs, near)
    pair = kernel(pair_kernel, "pair", shape((2, ROWS), f32), [VMEM] * 2 + [ANY], flops=LONG)(mine, core, send)
    plane = partner(pair)
    keep, send = kernel(
        join_kernel, "rows_joined", (shape((TOK, HD), f32), shape((TOK, HD), bf16)), [VMEM] * 5, flops=LONG
    )(probs, near, across(send), mine, core)
    got = partner(send)
    cols = kernel(
        column_kernel, "columns", shape((BLOCKS * NZL, HALF), f32), [VMEM] * 4 + [ANY], flops=LONG
    )(probs, mine, pair, plane, send)
    parts = lax.all_to_all(cols.reshape(BLOCKS * NZL, 1, HALF), ("y", "x", "zl"), 0, 0, tiled=True)
    rows = kernel(merge_kernel, "merge", shape((TOK, HD), bf16), [VMEM] * 4, flops=LONG)(keep, got, pair, plane)
    parts, _ = lax.optimization_barrier((parts, rows))
    piece = lax.dynamic_slice_in_dim(parts.reshape(BLOCKS * NZL, HALF), lax.axis_index("zl") * CHUNK, CHUNK, axis=1)
    return rows, jnp.sum(piece, axis=0) / HEADS


def solution(mesh):
    fine = Mesh(mesh.devices.reshape(tuple(AXES.values())), tuple(AXES))
    ctx, head = ("y", "zh", "x"), ("zl", "c")
    return jax.shard_map(
        body,
        mesh=fine,
        in_specs=(P(ctx, head), P(ctx, None), P(ctx, None), P()),
        out_specs=(P(ctx, head), P(ctx + head)),
        check_vma=False,
    )
```

```python
import math

import jax
import jax.numpy as jnp
from jax import lax
from jax.experimental import pallas as pl
from jax.experimental.pallas import tpu as pltpu
from jax.sharding import Mesh, PartitionSpec as P

HD = 128
HEADS = 8
AXES = {"y": 4, "zh": 2, "x": 4, "zl": 4, "c": 2}
NX = AXES["x"]
NZL = AXES["zl"]
TOK = 256
CHUNK = TOK // HEADS
HALF = TOK // 2
BLOCKS = AXES["y"] * NX
ORDER = [y * NX + x for y in (0, 2, 1, 3) for x in range(NX)]
KEYS = BLOCKS * HALF
FLIPS = 4
ROWS = FLIPS * TOK
TILE = 512
SCALE = math.log2(math.e) / math.sqrt(HD)
OWN, OTHER = 4, 5
BARRED = 32768.0
LONG = 20_000_000_000
MIB = 1024 * 1024
VMEM = pl.BlockSpec(memory_space=pltpu.VMEM)
ANY = pl.BlockSpec(memory_space=pl.ANY)
SMEM = pl.BlockSpec(memory_space=pltpu.SMEM)


def spread_kernel(keys_ref, values_ref, out_ref, piece_ref, in_sems, out_sems):
    c = lax.axis_index("c")
    reads = [
        pltpu.make_async_copy(ref.at[:, c], piece_ref.at[n], in_sems.at[n])
        for n, ref in enumerate((keys_ref, values_ref))
    ]
    for copy in reads:
        copy.start()
    for copy in reads:
        copy.wait()
    writes = [pltpu.make_async_copy(piece_ref, out_ref.at[i], out_sems.at[i]) for i in range(BLOCKS)]
    for copy in writes:
        copy.start()
    for copy in writes:
        copy.wait()


def swapped(major):
    return major % 2 * 2 + major // 2


def inside_block(index):
    return (index // CHUNK * 2 + lax.axis_index("c")) * CHUNK + index % CHUNK


def limit_kernel(docs_ref, own_ref, q_ref, row_mask_ref, key_mask_ref):
    q_ref[...] = own_ref[...]
    y, zh, x = (lax.axis_index(a) for a in ("y", "zh", "x"))
    own, other = y * 8 + zh * 4 + x, y * 8 + (1 - zh) * 4 + x
    ends = [docs_ref[0]]
    for i in (1, 2):
        ends.append(ends[-1] + docs_ref[i])

    def document(pos):
        return sum((pos >= end).astype(jnp.int32) for end in ends)

    row = lax.broadcasted_iota(jnp.int32, (ROWS, HD), 0)
    lane = lax.broadcasted_iota(jnp.int32, (ROWS, HD), 1)
    mine = row < 2 * TOK
    doc = document(jnp.where(mine, own, other) * TOK + row % TOK)
    hit = (lane == doc) | (lane == jnp.where(mine, OWN, OTHER))
    row_mask_ref[...] = jnp.where(hit, 1.0, 0.0).astype(jnp.bfloat16)

    key = lax.broadcasted_iota(jnp.int32, (KEYS, HD), 0)
    lane = lax.broadcasted_iota(jnp.int32, (KEYS, HD), 1)
    slot = key // HALF
    block = swapped(slot // NX) * 8 + zh * 4 + slot % NX
    doc = document(block * TOK + inside_block(key % HALF))
    barred = (lane < OWN) & (lane != doc)
    barred = barred | ((lane == OWN) & (block >= own)) | ((lane == OTHER) & (block > other))
    key_mask_ref[...] = jnp.where(barred, -BARRED, 0.0).astype(jnp.bfloat16)


def score_kernel(near_ref, q0, q1, q2, q3, row_mask_ref, key_mask_ref, probs_ref, stats_ref, raw_ref):
    across_depth = (((1,), (1,)), ((), ()))
    queries = jnp.concatenate([q[...] for q in (q0, q1, q2, q3)], axis=0)
    queries = jnp.concatenate([queries, row_mask_ref[...]], axis=1)
    own = 2 * TOK
    slot = swapped(lax.axis_index("y")) * NX + lax.axis_index("x")
    mask = key_mask_ref[pl.ds(pl.multiple_of(slot * HALF, HALF), HALF), :]
    feature = lax.broadcasted_iota(jnp.int32, (HALF, HD), 1)
    mask = jnp.where(feature == OWN, 0.0, mask.astype(jnp.float32)).astype(jnp.bfloat16)
    block = jnp.concatenate([near_ref[slot, 0], mask], axis=1)
    diagonal = lax.dot_general(queries[:own], block, across_depth, preferred_element_type=jnp.float32)
    row = lax.broadcasted_iota(jnp.int32, (own, HALF), 0) % TOK
    lane = lax.broadcasted_iota(jnp.int32, (own, HALF), 1)
    diagonal = jnp.where(inside_block(lane) <= row, diagonal, -jnp.inf)
    peak = jnp.maximum(jnp.full((own, HALF), -1e30, jnp.float32), diagonal)
    peak = jnp.concatenate([peak, jnp.full((ROWS - own, HALF), -1e30, jnp.float32)], axis=0)
    per = TILE // HALF
    for t in range(KEYS // TILE):
        block = near_ref[t * per : (t + 1) * per, 0].reshape(TILE, HD)
        block = jnp.concatenate([block, key_mask_ref[t * TILE : (t + 1) * TILE, :]], axis=1)
        raw = lax.dot_general(queries, block, across_depth, preferred_element_type=jnp.float32)
        for j in range(per):
            part = raw[:, j * HALF : (j + 1) * HALF]
            first = t * TILE + j * HALF
            raw_ref[:, first : first + HALF] = part
            peak = jnp.maximum(peak, part)
    raw_ref[0:own, pl.ds(pl.multiple_of(slot * HALF, HALF), HALF)] = diagonal
    row_max = jnp.max(peak, axis=1, keepdims=True)
    total = jnp.zeros((ROWS, HALF), jnp.float32)
    for j in range(0, KEYS, HALF):
        probs = jnp.exp2((raw_ref[:, j : j + HALF] - row_max) * SCALE)
        probs_ref[:, j : j + HALF] = probs.astype(jnp.bfloat16)
        total = total + probs
    row_sum = jnp.sum(total, axis=1, keepdims=True)
    first_lane = lax.broadcasted_iota(jnp.int32, (ROWS, HALF), 1) == 0
    stats_ref[...] = jnp.where(first_lane, row_max, row_sum).T[0:2, :]


def weighted(probs_ref, near_ref, k):
    values = near_ref[:, 1].reshape(KEYS, HD)
    return jnp.dot(probs_ref[k * TOK : (k + 1) * TOK, :], values, preferred_element_type=jnp.float32)


def send_kernel(probs_ref, near_ref, send_ref):
    for k in range(2):
        send_ref[k] = weighted(probs_ref, near_ref, 2 * k + 1).astype(jnp.bfloat16)


def stat(ref, k):
    cut = slice(k * TOK, (k + 1) * TOK)
    return ref[0:1, cut], ref[1:2, cut]


def as_column(row):
    return jnp.broadcast_to(row, (HD, TOK)).T


def pair_kernel(mine_ref, core_ref, send_ref, pair_ref):
    for k in range(FLIPS):
        (m0, l0), (m1, l1) = stat(mine_ref, k), stat(core_ref, k ^ 1)
        top = jnp.maximum(m0, m1)
        cut = slice(k * TOK, (k + 1) * TOK)
        pair_ref[0:1, cut] = top
        pair_ref[1:2, cut] = l0 * jnp.exp2((m0 - top) * SCALE) + l1 * jnp.exp2((m1 - top) * SCALE)


def join_kernel(probs_ref, near_ref, got_ref, mine_ref, core_ref, keep_ref, send_ref):
    for k, ref in ((0, keep_ref), (2, send_ref)):
        m0, m1 = stat(mine_ref, k)[0], stat(core_ref, k ^ 1)[0]
        top = jnp.maximum(m0, m1)
        w0, w1 = jnp.exp2((m0 - top) * SCALE), jnp.exp2((m1 - top) * SCALE)
        joined = weighted(probs_ref, near_ref, k) * as_column(w0) + got_ref[k // 2].astype(jnp.float32) * as_column(w1)
        ref[...] = joined.astype(ref.dtype)


def column_kernel(probs_ref, mine_ref, pair_ref, plane_ref, send_ref, cols_ref):
    weight = []
    for k in range(FLIPS):
        (m0, l0), (m1, l1) = stat(pair_ref, k), stat(plane_ref, k ^ 2)
        top = jnp.maximum(m0, m1)
        norm = l0 * jnp.exp2((m0 - top) * SCALE) + l1 * jnp.exp2((m1 - top) * SCALE)
        weight.append(jnp.exp2((stat(mine_ref, k)[0] - top) * SCALE) / norm)
    weight = jnp.concatenate(weight, axis=1)
    high = weight.astype(jnp.bfloat16).astype(jnp.float32)
    row = lax.broadcasted_iota(jnp.int32, (8, ROWS), 0)
    both = jnp.where(row == 0, high, jnp.where(row == 1, weight - high, 0.0)).astype(jnp.bfloat16)
    for b in range(0, BLOCKS, 2):
        first = b * HALF
        sums = jnp.dot(both, probs_ref[:, first : first + 2 * HALF], preferred_element_type=jnp.float32)
        line = jnp.sum(sums, axis=0, keepdims=True)
        pair = [jnp.broadcast_to(line[:, i * HALF : (i + 1) * HALF], (NZL, HALF)) for i in range(2)]
        source = swapped(b // NX) * NX + b % NX
        cols_ref[source * NZL : (source + 2) * NZL, :] = jnp.concatenate(pair, axis=0)


def merge_kernel(keep_ref, got_ref, pair_ref, plane_ref, out_ref):
    (m0, l0), (m1, l1) = stat(pair_ref, 0), stat(plane_ref, 2)
    top = jnp.maximum(m0, m1)
    w0, w1 = jnp.exp2((m0 - top) * SCALE), jnp.exp2((m1 - top) * SCALE)
    norm = w0 * l0 + w1 * l1
    out = keep_ref[...] * as_column(w0 / norm) + got_ref[...].astype(jnp.float32) * as_column(w1 / norm)
    out_ref[...] = out.astype(jnp.bfloat16)


def kernel(fn, name, shapes, specs, scratch=(), limit=8, space=VMEM, flops=0):
    return pl.pallas_call(
        fn,
        out_shape=shapes,
        in_specs=specs,
        out_specs=jax.tree.map(lambda _: space, shapes),
        scratch_shapes=scratch,
        compiler_params=pltpu.CompilerParams(vmem_limit_bytes=limit * MIB),
        cost_estimate=pl.CostEstimate(flops=flops, bytes_accessed=0, transcendentals=0) if flops else None,
        name=name,
    )


def body(queries, keys, values, doc_lengths):
    shape = jax.ShapeDtypeStruct
    f32, bf16 = jnp.float32, jnp.bfloat16
    def across(x):
        return lax.ppermute(x, "c", [(0, 1), (1, 0)])

    def partner(x):
        return lax.ppermute(x, ("zh", "zl", "c"), [(i, i ^ 12) for i in range(16)])

    copies = kernel(
        spread_kernel,
        "spread",
        shape((BLOCKS, 2, NZL, CHUNK, HD), bf16),
        [ANY] * 2,
        [
            pltpu.VMEM((2, NZL, CHUNK, HD), bf16),
            pltpu.SemaphoreType.DMA((2,)),
            pltpu.SemaphoreType.DMA((BLOCKS,)),
        ],
        limit=60,
        space=ANY,
    )(keys.reshape(NZL, 2, CHUNK, HD), values.reshape(NZL, 2, CHUNK, HD)).reshape(BLOCKS, 2, HALF, HD)
    near = lax.all_to_all(copies, ("y", "x"), 0, 0, axis_index_groups=[ORDER], tiled=True)
    q1, q2 = across(queries), partner(queries)
    q3 = across(q2)
    own, row_mask, key_mask = kernel(
        limit_kernel,
        "limits",
        (shape((TOK, HD), bf16), shape((ROWS, HD), bf16), shape((KEYS, HD), bf16)),
        [SMEM, VMEM],
    )(doc_lengths, queries)
    near, q1, q2, q3, own, row_mask, key_mask = lax.optimization_barrier(
        (near, q1, q2, q3, own, row_mask, key_mask)
    )
    probs, mine = kernel(
        score_kernel,
        "scores",
        (shape((ROWS, KEYS), bf16), shape((2, ROWS), f32)),
        [VMEM] * 7,
        [pltpu.VMEM((ROWS, KEYS), f32)],
        limit=24,
    )(near, own, q1, q2, q3, row_mask, key_mask)
    core = across(mine)
    send = kernel(send_kernel, "rows_sent", shape((2, TOK, HD), bf16), [VMEM] * 2, flops=LONG)(probs, near)
    pair = kernel(pair_kernel, "pair", shape((2, ROWS), f32), [VMEM] * 2 + [ANY], flops=LONG)(mine, core, send)
    plane = partner(pair)
    keep, send = kernel(
        join_kernel, "rows_joined", (shape((TOK, HD), f32), shape((TOK, HD), bf16)), [VMEM] * 5, flops=LONG
    )(probs, near, across(send), mine, core)
    got = partner(send)
    cols = kernel(
        column_kernel, "columns", shape((BLOCKS * NZL, HALF), f32), [VMEM] * 4 + [ANY], flops=LONG
    )(probs, mine, pair, plane, send)
    parts = lax.all_to_all(cols.reshape(BLOCKS * NZL, 1, HALF), ("y", "x", "zl"), 0, 0, tiled=True)
    rows = kernel(merge_kernel, "merge", shape((TOK, HD), bf16), [VMEM] * 4, flops=LONG)(keep, got, pair, plane)
    parts, _ = lax.optimization_barrier((parts, rows))
    piece = lax.dynamic_slice_in_dim(parts.reshape(BLOCKS * NZL, HALF), lax.axis_index("zl") * CHUNK, CHUNK, axis=1)
    return rows, jnp.sum(piece, axis=0) / HEADS


def solution(mesh):
    fine = Mesh(mesh.devices.reshape(tuple(AXES.values())), tuple(AXES))
    ctx, head = ("y", "zh", "x"), ("zl", "c")
    return jax.shard_map(
        body,
        mesh=fine,
        in_specs=(P(ctx, head), P(ctx, None), P(ctx, None), P()),
        out_specs=(P(ctx, head), P(ctx + head)),
        check_vma=False,
    )
```

```python
import math

import jax
import jax.numpy as jnp
from jax import lax
from jax.experimental import pallas as pl
from jax.experimental.pallas import tpu as pltpu
from jax.sharding import Mesh, PartitionSpec as P

HD = 128
HEADS = 8
AXES = {"y": 4, "zh": 2, "x": 4, "zl": 4, "c": 2}
NX = AXES["x"]
NZL = AXES["zl"]
TOK = 256
CHUNK = TOK // HEADS
HALF = TOK // 2
BLOCKS = AXES["y"] * NX
KEYS = BLOCKS * HALF
FLIPS = 4
ROWS = FLIPS * TOK
TILE = 1024
SCALE = math.log2(math.e) / math.sqrt(HD)
OWN, OTHER = 4, 5
BARRED = 32768.0
LONG = 20_000_000_000
MIB = 1024 * 1024
VMEM = pl.BlockSpec(memory_space=pltpu.VMEM)
ANY = pl.BlockSpec(memory_space=pl.ANY)
SMEM = pl.BlockSpec(memory_space=pltpu.SMEM)


def spread_kernel(keys_ref, values_ref, out_ref, piece_ref, in_sems, out_sems):
    c = lax.axis_index("c")
    reads = [
        pltpu.make_async_copy(ref.at[:, c], piece_ref.at[n], in_sems.at[n])
        for n, ref in enumerate((keys_ref, values_ref))
    ]
    for copy in reads:
        copy.start()
    for copy in reads:
        copy.wait()
    writes = [pltpu.make_async_copy(piece_ref, out_ref.at[i], out_sems.at[i]) for i in range(BLOCKS)]
    for copy in writes:
        copy.start()
    for copy in writes:
        copy.wait()


def inside_block(index):
    return (index // CHUNK * 2 + lax.axis_index("c")) * CHUNK + index % CHUNK


def limit_kernel(docs_ref, own_ref, q_ref, row_mask_ref, key_mask_ref):
    q_ref[...] = own_ref[...]
    y, zh, x = (lax.axis_index(a) for a in ("y", "zh", "x"))
    own, other = y * 8 + zh * 4 + x, y * 8 + (1 - zh) * 4 + x
    ends = [docs_ref[0]]
    for i in (1, 2):
        ends.append(ends[-1] + docs_ref[i])

    def document(pos):
        return sum((pos >= end).astype(jnp.int32) for end in ends)

    row = lax.broadcasted_iota(jnp.int32, (ROWS, HD), 0)
    lane = lax.broadcasted_iota(jnp.int32, (ROWS, HD), 1)
    mine = row < 2 * TOK
    doc = document(jnp.where(mine, own, other) * TOK + row % TOK)
    hit = (lane == doc) | (lane == jnp.where(mine, OWN, OTHER))
    row_mask_ref[...] = jnp.where(hit, 1.0, 0.0).astype(jnp.bfloat16)

    key = lax.broadcasted_iota(jnp.int32, (KEYS, HD), 0)
    lane = lax.broadcasted_iota(jnp.int32, (KEYS, HD), 1)
    slot = key // HALF
    block = slot // NX * 8 + zh * 4 + slot % NX
    doc = document(block * TOK + inside_block(key % HALF))
    barred = (lane < OWN) & (lane != doc)
    barred = barred | ((lane == OWN) & (block >= own)) | ((lane == OTHER) & (block > other))
    key_mask_ref[...] = jnp.where(barred, -BARRED, 0.0).astype(jnp.bfloat16)


def score_kernel(near_ref, q0, q1, q2, q3, row_mask_ref, key_mask_ref, probs_ref, stats_ref, raw_ref):
    across_depth = (((1,), (1,)), ((), ()))
    queries = jnp.concatenate([q[...] for q in (q0, q1, q2, q3)], axis=0)
    queries = jnp.concatenate([queries, row_mask_ref[...]], axis=1)
    own = 2 * TOK
    slot = lax.axis_index("y") * NX + lax.axis_index("x")
    mask = key_mask_ref[pl.ds(pl.multiple_of(slot * HALF, HALF), HALF), :]
    feature = lax.broadcasted_iota(jnp.int32, (HALF, HD), 1)
    mask = jnp.where(feature == OWN, 0.0, mask.astype(jnp.float32)).astype(jnp.bfloat16)
    block = jnp.concatenate([near_ref[slot, 0], mask], axis=1)
    diagonal = lax.dot_general(queries[:own], block, across_depth, preferred_element_type=jnp.float32)
    row = lax.broadcasted_iota(jnp.int32, (own, HALF), 0) % TOK
    lane = lax.broadcasted_iota(jnp.int32, (own, HALF), 1)
    diagonal = jnp.where(inside_block(lane) <= row, diagonal, -jnp.inf)
    peak = jnp.maximum(jnp.full((own, HALF), -1e30, jnp.float32), diagonal)
    peak = jnp.concatenate([peak, jnp.full((ROWS - own, HALF), -1e30, jnp.float32)], axis=0)
    per = TILE // HALF
    for t in range(KEYS // TILE):
        block = near_ref[t * per : (t + 1) * per, 0].reshape(TILE, HD)
        block = jnp.concatenate([block, key_mask_ref[t * TILE : (t + 1) * TILE, :]], axis=1)
        raw = lax.dot_general(queries, block, across_depth, preferred_element_type=jnp.float32)
        for j in range(per):
            part = raw[:, j * HALF : (j + 1) * HALF]
            first = t * TILE + j * HALF
            raw_ref[:, first : first + HALF] = part
            peak = jnp.maximum(peak, part)
    raw_ref[0:own, pl.ds(pl.multiple_of(slot * HALF, HALF), HALF)] = diagonal
    row_max = jnp.max(peak, axis=1, keepdims=True)
    total = jnp.zeros((ROWS, HALF), jnp.float32)
    for j in range(0, KEYS, HALF):
        probs = jnp.exp2((raw_ref[:, j : j + HALF] - row_max) * SCALE)
        probs_ref[:, j : j + HALF] = probs.astype(jnp.bfloat16)
        total = total + probs
    row_sum = jnp.sum(total, axis=1, keepdims=True)
    first_lane = lax.broadcasted_iota(jnp.int32, (ROWS, HALF), 1) == 0
    stats_ref[...] = jnp.where(first_lane, row_max, row_sum).T[0:2, :]


def weighted(probs_ref, near_ref, k):
    values = near_ref[:, 1].reshape(KEYS, HD)
    return jnp.dot(probs_ref[k * TOK : (k + 1) * TOK, :], values, preferred_element_type=jnp.float32)


def send_kernel(probs_ref, near_ref, send_ref):
    for k in range(2):
        send_ref[k] = weighted(probs_ref, near_ref, 2 * k + 1).astype(jnp.bfloat16)


def stat(ref, k):
    cut = slice(k * TOK, (k + 1) * TOK)
    return ref[0:1, cut], ref[1:2, cut]


def as_column(row):
    return jnp.broadcast_to(row, (HD, TOK)).T


def pair_kernel(mine_ref, core_ref, send_ref, pair_ref):
    for k in range(FLIPS):
        (m0, l0), (m1, l1) = stat(mine_ref, k), stat(core_ref, k ^ 1)
        top = jnp.maximum(m0, m1)
        cut = slice(k * TOK, (k + 1) * TOK)
        pair_ref[0:1, cut] = top
        pair_ref[1:2, cut] = l0 * jnp.exp2((m0 - top) * SCALE) + l1 * jnp.exp2((m1 - top) * SCALE)


def join_kernel(probs_ref, near_ref, got_ref, mine_ref, core_ref, keep_ref, send_ref):
    for k, ref in ((0, keep_ref), (2, send_ref)):
        m0, m1 = stat(mine_ref, k)[0], stat(core_ref, k ^ 1)[0]
        top = jnp.maximum(m0, m1)
        w0, w1 = jnp.exp2((m0 - top) * SCALE), jnp.exp2((m1 - top) * SCALE)
        joined = weighted(probs_ref, near_ref, k) * as_column(w0) + got_ref[k // 2].astype(jnp.float32) * as_column(w1)
        ref[...] = joined.astype(ref.dtype)


def column_kernel(probs_ref, mine_ref, pair_ref, plane_ref, send_ref, cols_ref):
    weight = []
    for k in range(FLIPS):
        (m0, l0), (m1, l1) = stat(pair_ref, k), stat(plane_ref, k ^ 2)
        top = jnp.maximum(m0, m1)
        norm = l0 * jnp.exp2((m0 - top) * SCALE) + l1 * jnp.exp2((m1 - top) * SCALE)
        weight.append(jnp.exp2((stat(mine_ref, k)[0] - top) * SCALE) / norm)
    weight = jnp.concatenate(weight, axis=1)
    high = weight.astype(jnp.bfloat16).astype(jnp.float32)
    row = lax.broadcasted_iota(jnp.int32, (8, ROWS), 0)
    both = jnp.where(row == 0, high, jnp.where(row == 1, weight - high, 0.0)).astype(jnp.bfloat16)
    for b in range(0, BLOCKS, 2):
        first = b * HALF
        sums = jnp.dot(both, probs_ref[:, first : first + 2 * HALF], preferred_element_type=jnp.float32)
        line = jnp.sum(sums, axis=0, keepdims=True)
        pair = [jnp.broadcast_to(line[:, i * HALF : (i + 1) * HALF], (NZL, HALF)) for i in range(2)]
        cols_ref[b * NZL : (b + 2) * NZL, :] = jnp.concatenate(pair, axis=0)


def merge_kernel(keep_ref, got_ref, pair_ref, plane_ref, out_ref):
    (m0, l0), (m1, l1) = stat(pair_ref, 0), stat(plane_ref, 2)
    top = jnp.maximum(m0, m1)
    w0, w1 = jnp.exp2((m0 - top) * SCALE), jnp.exp2((m1 - top) * SCALE)
    norm = w0 * l0 + w1 * l1
    out = keep_ref[...] * as_column(w0 / norm) + got_ref[...].astype(jnp.float32) * as_column(w1 / norm)
    out_ref[...] = out.astype(jnp.bfloat16)


def kernel(fn, name, shapes, specs, scratch=(), limit=8, space=VMEM, flops=0):
    return pl.pallas_call(
        fn,
        out_shape=shapes,
        in_specs=specs,
        out_specs=jax.tree.map(lambda _: space, shapes),
        scratch_shapes=scratch,
        compiler_params=pltpu.CompilerParams(vmem_limit_bytes=limit * MIB),
        cost_estimate=pl.CostEstimate(flops=flops, bytes_accessed=0, transcendentals=0) if flops else None,
        name=name,
    )


def body(queries, keys, values, doc_lengths):
    shape = jax.ShapeDtypeStruct
    f32, bf16 = jnp.float32, jnp.bfloat16
    def across(x):
        return lax.ppermute(x, "c", [(0, 1), (1, 0)])

    def partner(x):
        return lax.ppermute(x, ("zh", "zl", "c"), [(i, i ^ 12) for i in range(16)])

    copies = kernel(
        spread_kernel,
        "spread",
        shape((BLOCKS, 2, NZL, CHUNK, HD), bf16),
        [ANY] * 2,
        [
            pltpu.VMEM((2, NZL, CHUNK, HD), bf16),
            pltpu.SemaphoreType.DMA((2,)),
            pltpu.SemaphoreType.DMA((BLOCKS,)),
        ],
        limit=60,
        space=ANY,
    )(keys.reshape(NZL, 2, CHUNK, HD), values.reshape(NZL, 2, CHUNK, HD)).reshape(BLOCKS, 2, HALF, HD)
    near = lax.all_to_all(copies, ("y", "x"), 0, 0, tiled=True)
    q1, q2 = across(queries), partner(queries)
    q3 = across(q2)
    own, row_mask, key_mask = kernel(
        limit_kernel,
        "limits",
        (shape((TOK, HD), bf16), shape((ROWS, HD), bf16), shape((KEYS, HD), bf16)),
        [SMEM, VMEM],
    )(doc_lengths, queries)
    near, q1, q2, q3, own, row_mask, key_mask = lax.optimization_barrier(
        (near, q1, q2, q3, own, row_mask, key_mask)
    )
    probs, mine = kernel(
        score_kernel,
        "scores",
        (shape((ROWS, KEYS), bf16), shape((2, ROWS), f32)),
        [VMEM] * 7,
        [pltpu.VMEM((ROWS, KEYS), f32)],
        limit=24,
    )(near, own, q1, q2, q3, row_mask, key_mask)
    core = across(mine)
    send = kernel(send_kernel, "rows_sent", shape((2, TOK, HD), bf16), [VMEM] * 2, flops=LONG)(probs, near)
    pair = kernel(pair_kernel, "pair", shape((2, ROWS), f32), [VMEM] * 2 + [ANY], flops=LONG)(mine, core, send)
    plane = partner(pair)
    keep, send = kernel(
        join_kernel, "rows_joined", (shape((TOK, HD), f32), shape((TOK, HD), bf16)), [VMEM] * 5, flops=LONG
    )(probs, near, across(send), mine, core)
    got = partner(send)
    cols = kernel(
        column_kernel, "columns", shape((BLOCKS * NZL, HALF), f32), [VMEM] * 4 + [ANY], flops=LONG
    )(probs, mine, pair, plane, send)
    parts = lax.all_to_all(cols.reshape(BLOCKS * NZL, 1, HALF), ("y", "x", "zl"), 0, 0, tiled=True)
    rows = kernel(merge_kernel, "merge", shape((TOK, HD), bf16), [VMEM] * 4, flops=LONG)(keep, got, pair, plane)
    parts, _ = lax.optimization_barrier((parts, rows))
    piece = lax.dynamic_slice_in_dim(parts.reshape(BLOCKS * NZL, HALF), lax.axis_index("zl") * CHUNK, CHUNK, axis=1)
    return rows, jnp.sum(piece, axis=0) / HEADS


def solution(mesh):
    fine = Mesh(mesh.devices.reshape(tuple(AXES.values())), tuple(AXES))
    ctx, head = ("y", "zh", "x"), ("zl", "c")
    return jax.shard_map(
        body,
        mesh=fine,
        in_specs=(P(ctx, head), P(ctx, None), P(ctx, None), P()),
        out_specs=(P(ctx, head), P(ctx + head)),
        check_vma=False,
    )
```
